512 devices in a mesh: gx: 4 (over x), gy: 8 (over y_lo, core), gz: 16 (over y_hi, z).
Axes of the slice: x: 4, y: 8 (y_hi: 2, y_lo: 4; y = y_hi * 4 + y_lo), z: 8, core: 2. Of those that a mesh axis runs over, the one named last changes fastest.
Arguments:
- coarse_state: float32 [4, 32, 64, 2048], P(None, 'gx', 'gy', 'gz'), may hold values from -6 to 6
- diffusion_number: float32 [32, 64, 2048], P('gx', 'gy', 'gz'), may hold values from 0.01 to 0.15
- route_cell: int32 [4, 8, 16, 16], P('gx', 'gy', 'gz'), may hold values from -1 to 127, as said below
- fine_state: float32 [4, 8, 16, 16, 4, 4096], P('gx', 'gy', 'gz'), may hold values from -6 to 6
- fine_diffusion: float32 [4, 8, 16, 16, 4096], P('gx', 'gy', 'gz'), may hold values from 0.01 to 0.15
Outputs:
- coarse_next: float32 [4, 32, 64, 2048], P(None, 'gx', 'gy', 'gz')
- fine_next: float32 [4, 8, 16, 16, 4, 4096], P('gx', 'gy', 'gz')
The draws below stay inside these ranges and needn't reach their ends.
Inputs may be any that keep to these rules, and one draw needn't show every extreme that they name: `route_cell`: entry [a, b, s, h] is -1 where the source device (a, b, s) places no patch on host h of its gz line, else the index of the patch's block of 4^3 coarse cells among the source's (2) (2) (32) blocks, numbered with the third dimension fastest. The blocks named by one source are distinct.
All inputs are finite; a program needn't handle non-finite values.
Results may differ from the reference program's by a relative error of at most 0.000071.
Values sent between devices are 32-bit elements; how exact they have to be, the bound alone decides.
No kernel may reach another device: no remote copies, remote signals or barrier semaphores. Data moves between devices by JAX's collectives and lax.ppermute only.
A program may use at most 64 MiB of HBM per device.

```python
import math
import jax
import jax.numpy as jnp
import numpy as np
from jax import lax

NQ = 4
PB = 4
RATIO = 4
CX = 8
CY = 8
CZ = 128
FINE = 4096
NX = 32
NY = 64
NZ = 2048
N_GX = 4
N_GY = 8
N_GZ = 16


def draw_route_cell(key, part):
    key = jax.random.fold_in(key, 7)
    level_key, roll_key, order_key = jax.random.split(key, 3)
    block_count = CX // PB * (CY // PB) * (CZ // PB)
    levels = jax.random.randint(level_key, (N_GX, N_GY, 1, N_GZ), 0, 5)
    rolls = jax.random.randint(roll_key, (N_GX, N_GY, N_GZ, N_GZ), 0, 4)
    placed = rolls < levels
    placed = placed.at[0, 0, 0, 0].set(True).at[0, 0, 0, 1].set(False)
    scores = jax.random.randint(order_key, (N_GX, N_GY, N_GZ, block_count), 0, 2 ** 30 // block_count) * block_count
    scores = scores + jnp.arange(block_count, dtype=jnp.int32)
    scores = scores.at[0, 0, 0, block_count - 1].set(-1)
    ordering = jnp.argsort(scores, axis=-1).astype(jnp.int32)
    return jnp.where(placed, ordering[..., :N_GZ], -1).astype(jnp.int32)


def level_of(own_key, extent, pieces, smallest, top_value):
    def one(axis_at, shards_of):
        steps = jax.random.uniform(jax.random.fold_in(jax.random.fold_in(own_key, 6), axis_at), (shards_of,), jnp.float32, smallest / len(pieces), top_value / len(pieces))
        return jnp.repeat(jnp.exp(steps), extent[axis_at] // shards_of).reshape((-1,) + (1,) * (len(extent) - axis_at - 1))

    loudness = one(*pieces[0])
    for cut in pieces[1:]:
        loudness = loudness * one(*cut)
    return loudness


def centred(rng, dims, spread, bound, pieces=(), held_as=jnp.bfloat16):
    drawn = spread * jax.random.normal(rng, dims, jnp.float32)
    if pieces:
        drawn = drawn * level_of(rng, dims, pieces, -0.22, 0.18)
    return jnp.clip(drawn, -bound, bound).astype(held_as)


def setup_inputs(seed: int = 0) -> dict:
    arg_keys = jax.random.split(jax.random.key(seed), 6)
    return {
        "coarse_state": centred(arg_keys[0], (NQ, NX, NY, NZ), 1.0, 6.0, ((1, 4), (2, 8), (3, 16)), jnp.float32),
        "diffusion_number": jnp.clip(jnp.exp(math.log(0.15) - 2.7080503 * jax.random.uniform(arg_keys[1], (NX, NY, NZ), jnp.float32) ** level_of(arg_keys[1], (NX, NY, NZ), ((0, 4), (1, 8), (2, 16)), -0.2, 0.2)), 0.01, 0.15),
        "route_cell": draw_route_cell(jax.random.fold_in(arg_keys[5], 71), 0),
        "fine_state": centred(arg_keys[3], (N_GX, N_GY, N_GZ, N_GZ, NQ, FINE), 1.0, 6.0, ((0, 4), (1, 8), (2, 16)), jnp.float32),
        "fine_diffusion": jnp.clip(jnp.exp(math.log(0.15) - 2.7080503 * jax.random.uniform(arg_keys[4], (N_GX, N_GY, N_GZ, N_GZ, FINE), jnp.float32) ** level_of(arg_keys[4], (N_GX, N_GY, N_GZ, N_GZ, FINE), ((0, 4), (1, 8), (2, 16)), -0.2, 0.2)), 0.01, 0.15),
    }


WIND_COARSE = (0.05, 0.03, 0.07)
HIGHEST = lax.Precision.HIGHEST


def shifted(padded, axis_number, offset):
    interior = [padded.shape[-3] - 4, padded.shape[-2] - 4, padded.shape[-1] - 4]
    anchor_list = [2, 2, 2]
    anchor_list[axis_number] = 2 + offset
    return padded[..., anchor_list[0]:anchor_list[0] + interior[0], anchor_list[1]:anchor_list[1] + interior[1], anchor_list[2]:anchor_list[2] + interior[2]]


def scalar_rate(padded, number, wind_speeds):
    center = shifted(padded, 0, 0)
    laplace = -6.0 * center
    advect = jnp.zeros_like(center)
    for axis_number in range(3):
        forward = shifted(padded, axis_number, 1)
        backward = shifted(padded, axis_number, -1)
        laplace = laplace + forward + backward
        far_part = shifted(padded, axis_number, 2) - shifted(padded, axis_number, -2)
        advect = advect + wind_speeds[axis_number] * (8.0 * (forward - backward) - far_part) / 12.0
    return number * laplace - advect


def interp_table(coarse_count, ratio):
    fine_total = coarse_count * ratio + 4
    weights_table = np.zeros((fine_total, coarse_count + 4), np.float32)
    for fine_index in range(fine_total):
        position = (fine_index - 1.5) / ratio + 2.0
        first_node = math.floor(position - 0.5) - 1
        for offset in range(4):
            weight = 1.0
            for other_node in range(4):
                if other_node != offset:
                    weight = weight * (position - (first_node + other_node + 0.5)) / (offset - other_node)
            weights_table[fine_index, first_node + offset] = weight
    return weights_table


def prolong(coarse_block, weights_table):
    step_one = jnp.einsum("ai,qijk->qajk", weights_table, coarse_block, precision=HIGHEST)
    step_two = jnp.einsum("bj,qajk->qabk", weights_table, step_one, precision=HIGHEST)
    return jnp.einsum("ck,qabk->qabc", weights_table, step_two, precision=HIGHEST)


def fine_rate(fine_cube, ghost, number):
    padded = ghost.at[:, 2:-2, 2:-2, 2:-2].set(fine_cube)
    return scalar_rate(padded, number, tuple(RATIO * coarse_speed for coarse_speed in WIND_COARSE))


def reference(coarse_state, diffusion_number, route_cell, fine_state, fine_diffusion):
    pad_width = ((0, 0), (2, 2), (2, 2), (2, 2))

    def coarse_rate(coarse_field):
        padded = jnp.pad(coarse_field, pad_width)
        rates = lax.map(lambda single: scalar_rate(single, diffusion_number, WIND_COARSE), padded)
        return padded, rates

    padded_now, rate_now = coarse_rate(coarse_state)
    coarse_half = coarse_state + rate_now
    padded_half, rate_half = coarse_rate(coarse_half)
    coarse_full = 0.5 * (coarse_state + coarse_half + rate_half)

    fine_edge = PB * RATIO
    weights_table = jnp.asarray(interp_table(PB, RATIO)).astype(coarse_state.dtype)
    blocks_y = CY // PB
    blocks_z = CZ // PB
    slot_shape = (N_GX, N_GY, N_GZ, N_GZ)
    slot_cells = jnp.transpose(route_cell, (0, 1, 3, 2)).reshape(-1).astype(jnp.int32)
    along_x = lax.broadcasted_iota(jnp.int32, slot_shape, 0).reshape(-1)
    along_y = lax.broadcasted_iota(jnp.int32, slot_shape, 1).reshape(-1)
    along_s = lax.broadcasted_iota(jnp.int32, slot_shape, 3).reshape(-1)
    safe_cell = jnp.maximum(slot_cells, 0)
    corner_x = (along_x * CX + (safe_cell // (blocks_y * blocks_z)) * PB).astype(jnp.int32)
    corner_y = (along_y * CY + ((safe_cell // blocks_z) % blocks_y) * PB).astype(jnp.int32)
    corner_z = (along_s * CZ + (safe_cell % blocks_z) * PB).astype(jnp.int32)
    placed = slot_cells >= 0
    fine_flat = fine_state.reshape(-1, NQ, fine_edge ** 3)
    number_flat = fine_diffusion.reshape(-1, fine_edge ** 3)
    anchor = jnp.zeros((), jnp.int32)
    block_size = (NQ, PB + 4, PB + 4, PB + 4)

    def one_slot(inputs):
        start_x, start_y, start_z, fine_values, numbers = inputs
        starts = (anchor, start_x, start_y, start_z)
        block_now = lax.dynamic_slice(padded_now, starts, block_size)
        block_half = lax.dynamic_slice(padded_half, starts, block_size)
        fine_cube = fine_values.reshape(NQ, fine_edge, fine_edge, fine_edge)
        number = numbers.reshape(fine_edge, fine_edge, fine_edge)
        fine_half = fine_cube + fine_rate(fine_cube, prolong(block_now, weights_table), number)
        fine_done = 0.5 * (fine_cube + fine_half + fine_rate(fine_half, prolong(block_half, weights_table), number))
        averaged = fine_done.reshape(NQ, PB, RATIO, PB, RATIO, PB, RATIO).mean(axis=(2, 4, 6))
        return fine_done.reshape(NQ, fine_edge ** 3), averaged

    fine_full, averages = lax.map(one_slot, (corner_x, corner_y, corner_z, fine_flat, number_flat), batch_size=64)
    fine_next = jnp.where(placed[:, None, None], fine_full, fine_flat).reshape(fine_state.shape)

    def restrict(slot_index, coarse_field):
        starts = (anchor, corner_x[slot_index], corner_y[slot_index], corner_z[slot_index])
        current = lax.dynamic_slice(coarse_field, starts, (NQ, PB, PB, PB))
        return lax.dynamic_update_slice(coarse_field, jnp.where(placed[slot_index], averages[slot_index], current), starts)

    coarse_next = lax.fori_loop(0, slot_cells.shape[0], restrict, coarse_full)
    return coarse_next, fine_next
```

```python
import functools
import math

import jax
import jax.numpy as jnp
import numpy as np
from jax import lax
from jax.experimental import pallas as pl
from jax.experimental.pallas import tpu as pltpu
from jax.sharding import PartitionSpec as P

PB = 4
RATIO = 4
EDGE = PB * RATIO
HOSTS = 16
SLOT_ROWS = 40
WIND_COARSE = (0.05, 0.03, 0.07)
WIND_FINE = tuple(RATIO * speed for speed in WIND_COARSE)
F32 = jnp.float32
BF16 = jnp.bfloat16


def interp_table(coarse_count, ratio):
    fine_total = coarse_count * ratio + 4
    weights_table = np.zeros((fine_total, coarse_count + 4), np.float32)
    for fine_index in range(fine_total):
        position = (fine_index - 1.5) / ratio + 2.0
        first_node = math.floor(position - 0.5) - 1
        for offset in range(4):
            weight = 1.0
            for other_node in range(4):
                if other_node != offset:
                    weight = (
                        weight
                        * (position - (first_node + other_node + 0.5))
                        / (offset - other_node)
                    )
            weights_table[fine_index, first_node + offset] = weight
    return weights_table


def high_low(table):
    high = np.asarray(table, np.float32).astype(jnp.bfloat16)
    low = (np.asarray(table, np.float64) - high.astype(np.float64)).astype(jnp.bfloat16)
    return high, low


def tables():
    interp = interp_table(PB, RATIO).astype(np.float64)
    span = EDGE + 4
    lap = np.zeros((span, span, EDGE * EDGE))
    adv = np.zeros((span, span, EDGE * EDGE))
    for y in range(EDGE):
        for z in range(EDGE):
            col = y * EDGE + z
            lap[y + 2, z + 2, col] = -6.0
            for dy, dz, wind in ((1, 0, WIND_FINE[1]), (0, 1, WIND_FINE[2])):
                for sign in (1, -1):
                    lap[y + 2 + sign * dy, z + 2 + sign * dz, col] += 1.0
                    adv[y + 2 + sign * dy, z + 2 + sign * dz, col] += sign * 8.0 * wind / 12.0
                    adv[y + 2 + sign * 2 * dy, z + 2 + sign * 2 * dz, col] -= sign * wind / 12.0
    inner = np.zeros((span, span), bool)
    inner[2:-2, 2:-2] = True
    inner = inner.reshape(-1)
    both = np.concatenate([lap.reshape(span * span, -1), adv.reshape(span * span, -1)], axis=1)
    plane_hi, plane_lo = high_low(both[inner])
    plane = np.concatenate([plane_hi, plane_hi], axis=0)
    plane_rest = plane_lo[:, EDGE * EDGE :]
    spread = np.kron(interp, interp)
    ghost_hi, ghost_lo = high_low(spread.T @ np.where(inner[:, None], 0.0, both))
    ghost = np.concatenate([ghost_hi, ghost_lo, ghost_hi, np.zeros_like(ghost_hi)], axis=0)
    face_hi, face_lo = high_low(spread[inner].T)
    face = np.concatenate([face_hi, face_lo, face_hi, np.zeros_like(face_hi)], axis=0)
    mean = np.zeros((PB, EDGE, EDGE, PB, 4, PB, PB), np.float32)
    for big_x in range(PB):
        for y in range(EDGE):
            for z in range(EDGE):
                mean[big_x, y, z, z // RATIO, :, big_x, y // RATIO] = 1.0 / RATIO**3
    mean = mean.reshape(PB * EDGE * EDGE, 256).astype(jnp.bfloat16)
    copy = np.zeros((4, 2, PB, 2, PB, 2, 4, PB, PB), np.float32)
    for q in range(4):
        for big_x in range(PB):
            for big_y in range(PB):
                copy[q, :, big_x, :, big_y, 0, q, big_x, big_y] = 1.0
    copy = copy.reshape(256, 128).astype(jnp.bfloat16)
    return plane, plane_rest, ghost, face, mean, copy


def dot(left, right):
    return lax.dot_general(
        left, right, (((1,), (0,)), ((), ())), preferred_element_type=F32
    )


def dot_t(left, right):
    return lax.dot_general(
        left, right, (((1,), (1,)), ((), ())), preferred_element_type=F32
    )


def split(values):
    high = values.astype(BF16)
    return high, (values - high.astype(F32)).astype(BF16)


def ring_field(coarse_ref, number_ref, left_ref, right_ref, q, x):
    if x < 8:
        return coarse_ref[q, x] if q < 4 else number_ref[x]
    return right_ref[q, x - 8] if x < 12 else left_ref[q, x - 12]


def y_kernel(coarse_ref, number_ref, left_ref, right_ref, low_ref, high_ref):
    top = lax.broadcasted_iota(jnp.int32, (8, 128), 0) < 4
    field = functools.partial(ring_field, coarse_ref, number_ref, left_ref, right_ref)
    for q in range(5):
        for pair in range(8):
            even, odd = field(q, 2 * pair), field(q, 2 * pair + 1)
            at = pl.ds((q * 8 + pair) * 8, 8)
            low_ref[at] = jnp.where(top, even, pltpu.roll(odd, 4, 0))
            high_ref[at] = jnp.where(top, pltpu.roll(even, 4, 0), odd)


def z_kernel(
    coarse_ref, number_ref, left_ref, right_ref, below_ref, above_ref, all_ref, low_ref, high_ref
):
    top = lax.broadcasted_iota(jnp.int32, (8, 128), 0) < 4
    field = functools.partial(ring_field, coarse_ref, number_ref, left_ref, right_ref)
    for q in range(5):
        for pair in range(8):
            at = pl.ds((q * 8 + pair) * 8, 8)
            below, above = below_ref[at], above_ref[at]
            row = (q * 16 + 2 * pair) * 16
            all_ref[pl.ds(row, 8)] = field(q, 2 * pair)
            all_ref[pl.ds(row + 8, 8)] = jnp.where(top, above, pltpu.roll(below, 4, 0))
            all_ref[pl.ds(row + 16, 8)] = field(q, 2 * pair + 1)
            all_ref[pl.ds(row + 24, 8)] = jnp.where(top, pltpu.roll(above, 4, 0), below)
    group = lax.broadcasted_iota(jnp.int32, (40, 128), 1) // 4
    low = jnp.zeros((40, 128), F32)
    high = jnp.zeros((40, 128), F32)
    for g in range(32):
        rows = all_ref[pl.ds(g * 40, 40)]
        low = jnp.where(group == g, pltpu.roll(rows, 4 * g, 1) if g else rows, low)
        shift = (4 * g + 4) % 128
        high = jnp.where(group == g, pltpu.roll(rows, shift, 1) if shift else rows, high)
    low_ref[...] = low
    high_ref[...] = high


def slot_lanes(route_ref, width, shape):
    lane = lax.broadcasted_iota(jnp.int32, shape, 1)
    group = (lane // width) % HOSTS
    values = jnp.zeros(shape, jnp.int32)
    for slot in range(HOSTS):
        values = jnp.where(group == slot, route_ref[slot], values)
    return values


def rate_parts(center, x_near, x_far, y_axis, wind):
    rows, lanes = center.shape
    y_up, y_down = pltpu.roll(center, rows - 1, y_axis), pltpu.roll(center, 1, y_axis)
    y_up2, y_down2 = pltpu.roll(center, rows - 2, y_axis), pltpu.roll(center, 2, y_axis)
    z_up, z_down = pltpu.roll(center, lanes - 1, 1), pltpu.roll(center, 1, 1)
    z_up2, z_down2 = pltpu.roll(center, lanes - 2, 1), pltpu.roll(center, 2, 1)
    laplace = (
        (x_near[0] + x_near[1]) + (y_up + y_down) + (z_up + z_down) - 6.0 * center
    )
    advect = (
        (wind[0] / 12.0) * (8.0 * (x_near[0] - x_near[1]) - (x_far[0] - x_far[1]))
        + (wind[1] / 12.0) * (8.0 * (y_up - y_down) - (y_up2 - y_down2))
        + (wind[2] / 12.0) * (8.0 * (z_up - z_down) - (z_up2 - z_down2))
    )
    return laplace, advect


HALF_PLACES = tuple(range(10)) + (14, 15)
WINDOW_PLACES = (14, 15) + tuple(range(10))


def half_kernel(all_ref, before_ref, after_ref, route_ref, pay_ref, half_ref, now_ref, cut_ref):
    lane40 = lax.broadcasted_iota(jnp.int32, (40, 128), 1)
    before, after = before_ref[...], after_ref[...]
    for g in range(32):
        ahead = pltpu.roll(after, (128 - 4 * g) % 128, 1) if g else after
        shift = (124 - 4 * g) % 128
        behind = pltpu.roll(before, shift, 1) if shift else before
        rows = pl.ds(g * 40, 40)
        now_ref[rows, pl.ds(0, 128)] = all_ref[rows]
        now_ref[rows, pl.ds(128, 128)] = jnp.where(
            lane40 < 4, ahead, jnp.where(lane40 >= 124, behind, 0.0)
        )

    def sheet(q, x):
        return now_ref[pl.ds((q * 16 + x) * 16, 16)]

    for x in HALF_PLACES:
        number = sheet(4, x)
        for q in range(4):
            center = sheet(q, x)
            near = (sheet(q, (x + 1) % 16), sheet(q, (x - 1) % 16))
            far = (sheet(q, (x + 2) % 16), sheet(q, (x - 2) % 16))
            laplace, advect = rate_parts(center, near, far, 0, WIND_COARSE)
            stepped = center + number * laplace - advect
            half_ref[pl.ds((q * 16 + x) * 16, 16)] = jnp.where(number > 0.0, stepped, 0.0)

    cells = slot_lanes(route_ref, 8, (8, 128))[0:1]
    lane = lax.broadcasted_iota(jnp.int32, (1, 128), 1)
    wanted = (4 * (cells & 31) - 2 + (lane & 7)) & 255
    place = lax.broadcasted_iota(jnp.int32, (256, 128), 0)
    pick = jnp.where((place == wanted) & (cells >= 0), 1.0, 0.0).astype(BF16)
    far_x = jnp.broadcast_to(((cells >> 6) & 1) == 1, (16, 128))
    far_y = jnp.broadcast_to(((cells >> 5) & 1) == 1, (8, 128))
    for t, field_ref in enumerate((now_ref, half_ref)):
        for q in range(4):
            cut = []
            for first, count in ((14, 2), (0, 10)):
                high, low = split(field_ref[pl.ds((q * 16 + first) * 16, count * 16)])
                cut.append(dot(high, pick) + dot(low, pick))
            cut = jnp.concatenate(cut, axis=0)
            for i in range(8):
                rows = jnp.where(
                    far_x, cut[(i + 4) * 16 : (i + 5) * 16], cut[i * 16 : (i + 1) * 16]
                )
                near_rows = pltpu.roll(rows, 2, 0)[:8]
                far_rows = pltpu.roll(rows, 14, 0)[:8]
                cut_ref[pl.ds(((t * 4 + q) * 8 + i) * 8, 8)] = jnp.where(
                    far_y, far_rows, near_rows
                )
    group = lax.broadcasted_iota(jnp.int32, (32, 128), 1) // 8
    pieces = [
        cut_ref[pl.ds(t * 256 + y, 32, stride=8)] for t in range(2) for y in range(8)
    ]
    for step in (8, 4, 2, 1):
        swap = (group & step) != 0
        for i in range(16):
            if not i & step:
                a, b = pieces[i], pieces[i + step]
                pieces[i] = jnp.where(swap, pltpu.roll(b, 8 * step, 1), a)
                pieces[i + step] = jnp.where(swap, b, pltpu.roll(a, 128 - 8 * step, 1))
    for slot in range(HOSTS):
        pay_ref[pl.ds(slot * SLOT_ROWS, 32)] = pieces[slot]
        placed = jnp.where(route_ref[slot] >= 0, 1.0, 0.0)
        pay_ref[pl.ds(slot * SLOT_ROWS + 32, 8)] = jnp.full((8, 128), placed, F32)


def full_kernel(coarse_ref, number_ref, half_ref, route_ref, full_ref):
    lane = lax.broadcasted_iota(jnp.int32, (8, 128), 1)
    top = lax.broadcasted_iota(jnp.int32, (8, 128), 0) < 4
    covered = [jnp.zeros((8, 128), jnp.int32) for _ in range(4)]
    for slot in range(HOSTS):
        cell = route_ref[slot]
        hit = (lane // 4) == (cell & 31)
        for corner in range(4):
            chosen = jnp.where((cell >> 5) == corner, 1, 0)
            covered[corner] = jnp.where(hit, jnp.maximum(covered[corner], chosen), covered[corner])

    def sheet(q, x):
        return half_ref[pl.ds((q * 16 + x % 16) * 16, 16)]

    for x in range(8):
        keep = jnp.where(top, covered[(x // 4) * 2], covered[(x // 4) * 2 + 1]) == 0
        number = number_ref[x]
        for q in range(4):
            center = sheet(q, x)
            laplace, advect = rate_parts(
                center,
                (sheet(q, x + 1), sheet(q, x - 1)),
                (sheet(q, x + 2), sheet(q, x - 2)),
                0,
                WIND_COARSE,
            )
            done = 0.5 * (
                coarse_ref[q, x]
                + center[:8, :128]
                + number * laplace[:8, :128]
                - advect[:8, :128]
            )
            full_ref[q, x] = jnp.where(keep, done, 0.0)


def put_kernel(back_ref, full_ref, route_ref, copy_ref, next_ref):
    even = back_ref[pl.ds(0, 16, stride=2)]
    odd = back_ref[pl.ds(1, 16, stride=2)]
    values = jnp.concatenate(
        [even, pltpu.roll(even, 64, 1), odd, pltpu.roll(odd, 64, 1)], axis=0
    )
    high = values.astype(BF16)
    rest = values - high.astype(F32)
    low, lowest = split(rest)
    parts = jnp.concatenate([high, low, lowest, jnp.zeros_like(high)], axis=0)
    spread = dot_t(copy_ref[...], parts)
    cells = slot_lanes(route_ref, 1, (8, 256))[0:1]
    row = lax.broadcasted_iota(jnp.int32, (256, 1), 0)
    corner = ((row >> 5) & 1) * 2 + ((row >> 2) & 1)
    spread = jnp.where((cells >> 5) == corner, spread, 0.0).astype(BF16)
    z = lax.broadcasted_iota(jnp.int32, (128, 256), 0)
    lane = lax.broadcasted_iota(jnp.int32, (128, 256), 1)
    here = ((z >> 2) == (cells & 31)) & ((z & 3) == ((lane >> 4) & 3)) & (cells >= 0)
    added = dot_t(spread, jnp.where(here, 1.0, 0.0).astype(BF16))
    for q in range(4):
        for x in range(8):
            at = (q * 8 + x) * 8
            next_ref[q, x] = full_ref[q, x] + added[at : at + 8]


def plane_parts(field, plane_ref, rest_ref):
    high, low = split(field)
    both = dot(high, plane_ref[pl.ds(0, 256)]) + dot(low, plane_ref[pl.ds(256, 256)])
    return both[:, :256], both[:, 256:] + dot(high, rest_ref[...])


def x_parts(padded):
    laplace, advect = [], []
    for x in range(2, 18):
        laplace.append(padded[x + 1] + padded[x - 1])
        advect.append(
            (WIND_FINE[0] / 12.0)
            * (8.0 * (padded[x + 1] - padded[x - 1]) - (padded[x + 2] - padded[x - 2]))
        )
    return jnp.concatenate(laplace, axis=0), jnp.concatenate(advect, axis=0)


def load_numbers(number_ref):
    return jnp.concatenate(
        [number_ref[:, pl.ds(x * 256, 256)] for x in range(EDGE)], axis=0
    )


def early_kernel(fine_ref, number_ref, plane_ref, rest_ref, step_ref, field_ref):
    zero = jnp.zeros((HOSTS, 256), F32)
    numbers = load_numbers(number_ref)
    for q in range(4):
        planes = []
        for x in range(EDGE):
            sides = [
                fine_ref[pl.ds((2 * x + side) * 4 + q, HOSTS, stride=128)] for side in range(2)
            ]
            planes.append(jnp.concatenate(sides, axis=1))
        field = jnp.concatenate(planes, axis=0)
        laplace, advect = plane_parts(field, plane_ref, rest_ref)
        x_laplace, x_advect = x_parts([zero, zero] + planes + [zero, zero])
        at = pl.ds(q * 256, 256)
        field_ref[at] = field
        step_ref[at] = field + numbers * (laplace + x_laplace) - (advect + x_advect)


def late_kernel(
    block_ref,
    step_ref,
    field_ref,
    number_ref,
    plane_ref,
    rest_ref,
    ghost_ref,
    face_ref,
    mean_ref,
    fine_ref,
    back_ref,
):
    interp = interp_table(PB, RATIO)
    zero = jnp.zeros((HOSTS, 256), F32)
    numbers = load_numbers(number_ref)
    first_half = lax.broadcasted_iota(jnp.int32, (HOSTS, 128), 1) < 64
    placed = block_ref[pl.ds(32, HOSTS, stride=SLOT_ROWS)] > 0.5
    lane_q = (lax.broadcasted_iota(jnp.int32, (HOSTS, 256), 1) >> 4) & 3
    back = zero

    def ghosts(q, t):
        coarse = []
        for x in range(8):
            rows = block_ref[pl.ds(q * 8 + x, HOSTS, stride=SLOT_ROWS)]
            turned = pltpu.roll(rows, 64, 1)
            coarse.append(
                jnp.where(first_half, rows, turned) if t == 0 else jnp.where(first_half, turned, rows)
            )
        inner, outer = [], []
        for i in range(EDGE + 4):
            total = None
            for j in range(8):
                if interp[i, j] != 0.0:
                    term = float(interp[i, j]) * coarse[j]
                    total = term if total is None else total + term
            (inner if 2 <= i < EDGE + 2 else outer).append(total)
        inner = jnp.concatenate(inner, axis=0)
        outer = jnp.concatenate(outer, axis=0)
        sides = dot(jnp.concatenate(split(inner), axis=1), ghost_ref[...])
        faces = dot(jnp.concatenate(split(outer), axis=1), face_ref[...])
        return sides[:, :256], sides[:, 256:], [faces[i * 16 : (i + 1) * 16] for i in range(4)]

    for q in range(4):
        at = pl.ds(q * 256, 256)
        side_laplace, side_advect, faces = ghosts(q, 0)
        x_laplace, x_advect = x_parts(faces[:2] + [zero] * EDGE + faces[2:])
        half = step_ref[at] + numbers * (side_laplace + x_laplace) - (side_advect + x_advect)
        side_laplace, side_advect, faces = ghosts(q, 1)
        planes = [half[x * 16 : (x + 1) * 16] for x in range(EDGE)]
        x_laplace, x_advect = x_parts(faces[:2] + planes + faces[2:])
        laplace, advect = plane_parts(half, plane_ref, rest_ref)
        field = field_ref[at]
        done = 0.5 * (
            field
            + half
            + numbers * (laplace + side_laplace + x_laplace)
            - (advect + side_advect + x_advect)
        )
        sums = []
        for x in range(EDGE):
            rows = slice(x * 16, (x + 1) * 16)
            for side in range(2):
                lanes = slice(side * 128, side * 128 + 128)
                fine_ref[pl.ds((2 * x + side) * 4 + q, HOSTS, stride=128)] = jnp.where(
                    placed, done[rows, lanes], field[rows, lanes]
                )
        total = zero
        for big_x in range(PB):
            group = [done[(big_x * 4 + i) * 16 : (big_x * 4 + i + 1) * 16] for i in range(4)]
            sums.append((group[0] + group[1]) + (group[2] + group[3]))
        for big_x in range(PB):
            high, low = split(sums[big_x])
            weights = mean_ref[pl.ds(big_x * 256, 256)]
            total = total + dot(high, weights) + dot(low, weights)
        back = jnp.where(lane_q == q, total, back)
    back_ref[pl.ds(0, HOSTS, stride=2)] = back[:, :128]
    back_ref[pl.ds(1, HOSTS, stride=2)] = back[:, 128:]


def call(kernel, operands, outs, smem=(), scratch=(), flops=1000000, name=None):
    vmem = pl.BlockSpec(memory_space=pltpu.VMEM)
    scalar = pl.BlockSpec(memory_space=pltpu.SMEM)
    moved = sum(int(np.prod(o.shape)) * o.dtype.itemsize for o in operands)
    return pl.pallas_call(
        kernel,
        out_shape=tuple(jax.ShapeDtypeStruct(shape, F32) for shape in outs),
        in_specs=[scalar if i in smem else vmem for i in range(len(operands))],
        out_specs=tuple(vmem for _ in outs),
        scratch_shapes=[pltpu.VMEM(shape, F32) for shape in scratch],
        compiler_params=pltpu.CompilerParams(vmem_limit_bytes=40 * 1024 * 1024),
        cost_estimate=pl.CostEstimate(flops=flops, bytes_accessed=moved, transcendentals=0),
        name=name,
    )(*operands)


def shards(coarse_state, diffusion_number, route_cell, fine_state, fine_diffusion):
    plane, plane_rest, ghost, face, mean, copy = (jnp.asarray(table) for table in tables())
    route = route_cell.reshape(HOSTS)

    def exchange(low, high, axis):
        count = lax.axis_size(axis)
        up = [(i, i + 1) for i in range(count - 1)]
        down = [(i + 1, i) for i in range(count - 1)]
        return lax.ppermute(high, axis, up), lax.ppermute(low, axis, down)

    fields = jnp.concatenate([coarse_state, diffusion_number[None]], axis=0)
    left, right = exchange(fields[:, :4], fields[:, 4:], "gx")
    own = (coarse_state, diffusion_number, left, right)
    low, high = call(y_kernel, own, [(320, 128), (320, 128)], name="y_messages")
    below, above = exchange(low, high, "gy")
    everything, low, high = call(
        z_kernel, own + (below, above), [(1280, 128), (40, 128), (40, 128)], name="z_messages"
    )
    before, after = exchange(low, high, "gz")
    pay, half = call(
        half_kernel,
        (everything, before, after, route),
        [(HOSTS * SLOT_ROWS, 128), (1024, 256)],
        smem=(3,),
        scratch=[(1280, 256), (512, 128)],
        name="half_step",
    )
    fine_rows = fine_state.reshape(HOSTS, 4, 32, 128).transpose(0, 2, 1, 3).reshape(2048, 128)
    fine_numbers = fine_diffusion.reshape(HOSTS, EDGE**3)
    step, field = call(
        early_kernel,
        (fine_rows, fine_numbers, plane, plane_rest),
        [(1024, 256), (1024, 256)],
        flops=10**9,
        name="fine_early",
    )
    blocks = lax.all_to_all(
        pay.reshape(HOSTS, SLOT_ROWS, 128), "gz", split_axis=0, concat_axis=0, tiled=True
    ).reshape(HOSTS * SLOT_ROWS, 128)
    (full,) = call(
        full_kernel,
        (coarse_state, diffusion_number, half, route),
        [(4, 8, 8, 128)],
        smem=(3,),
        name="coarse_full",
    )
    fine_done, back = call(
        late_kernel,
        (blocks, step, field, fine_numbers, plane, plane_rest, ghost, face, mean),
        [(2048, 128), (32, 128)],
        flops=10**9,
        name="fine_late",
    )
    returned = lax.all_to_all(
        back.reshape(HOSTS, 2, 128), "gz", split_axis=0, concat_axis=0, tiled=True
    ).reshape(32, 128)
    (coarse_next,) = call(
        put_kernel,
        (returned, full, route, copy),
        [(4, 8, 8, 128)],
        smem=(2,),
        name="put_means",
    )
    fine_next = (
        fine_done.reshape(HOSTS, 32, 4, 128).transpose(0, 2, 1, 3).reshape(fine_state.shape)
    )
    return coarse_next, fine_next


def solution(mesh):
    return jax.shard_map(
        shards,
        mesh=mesh,
        in_specs=(
            P(None, "gx", "gy", "gz"),
            P("gx", "gy", "gz"),
            P("gx", "gy", "gz", None),
            P("gx", "gy", "gz", None, None, None),
            P("gx", "gy", "gz", None, None),
        ),
        out_specs=(P(None, "gx", "gy", "gz"), P("gx", "gy", "gz", None, None, None)),
        check_vma=False,
    )
```

```python
import functools
import math

import jax
import jax.numpy as jnp
import numpy as np
from jax import lax
from jax.experimental import pallas as pl
from jax.experimental.pallas import tpu as pltpu
from jax.sharding import PartitionSpec as P

PB = 4
RATIO = 4
EDGE = PB * RATIO
HOSTS = 16
LIMIT = 16
NUMBER_ROW = 32
MEAN_ROW = 64
FLAG_ROW = 66
SLOT_ROWS = 67
WIND_COARSE = (0.05, 0.03, 0.07)
WIND_FINE = tuple(RATIO * speed for speed in WIND_COARSE)
F32 = jnp.float32
BF16 = jnp.bfloat16


def interp_table(coarse_count, ratio):
    fine_total = coarse_count * ratio + 4
    weights_table = np.zeros((fine_total, coarse_count + 4), np.float32)
    for fine_index in range(fine_total):
        position = (fine_index - 1.5) / ratio + 2.0
        first_node = math.floor(position - 0.5) - 1
        for offset in range(4):
            weight = 1.0
            for other_node in range(4):
                if other_node != offset:
                    weight = (
                        weight
                        * (position - (first_node + other_node + 0.5))
                        / (offset - other_node)
                    )
            weights_table[fine_index, first_node + offset] = weight
    return weights_table


def high_low(table):
    high = np.asarray(table, np.float32).astype(jnp.bfloat16)
    low = (np.asarray(table, np.float64) - high.astype(np.float64)).astype(jnp.bfloat16)
    return high, low


def tables():
    interp = interp_table(PB, RATIO).astype(np.float64)
    span = EDGE + 4
    lap = np.zeros((span, span, EDGE * EDGE))
    adv = np.zeros((span, span, EDGE * EDGE))
    for y in range(EDGE):
        for z in range(EDGE):
            col = y * EDGE + z
            lap[y + 2, z + 2, col] = -6.0
            for dy, dz, wind in ((1, 0, WIND_FINE[1]), (0, 1, WIND_FINE[2])):
                for sign in (1, -1):
                    lap[y + 2 + sign * dy, z + 2 + sign * dz, col] += 1.0
                    adv[y + 2 + sign * dy, z + 2 + sign * dz, col] += sign * 8.0 * wind / 12.0
                    adv[y + 2 + sign * 2 * dy, z + 2 + sign * 2 * dz, col] -= sign * wind / 12.0
    inner = np.zeros((span, span), bool)
    inner[2:-2, 2:-2] = True
    inner = inner.reshape(-1)
    both = np.concatenate([lap.reshape(span * span, -1), adv.reshape(span * span, -1)], axis=1)
    plane_hi, plane_lo = high_low(both[inner])
    plane = np.concatenate([plane_hi, plane_hi], axis=0)
    plane_rest = plane_lo[:, EDGE * EDGE :]
    spread = np.kron(interp, interp)
    ghost_hi, ghost_lo = high_low(spread.T @ np.where(inner[:, None], 0.0, both))
    ghost = np.concatenate([ghost_hi, ghost_lo, ghost_hi, np.zeros_like(ghost_hi)], axis=0)
    face_hi, face_lo = high_low(spread[inner].T)
    face = np.concatenate([face_hi, face_lo, face_hi, np.zeros_like(face_hi)], axis=0)
    mean = np.zeros((PB, EDGE, EDGE, PB, 4, PB, PB), np.float32)
    for big_x in range(PB):
        for y in range(EDGE):
            for z in range(EDGE):
                mean[big_x, y, z, z // RATIO, :, big_x, y // RATIO] = 1.0 / RATIO**3
    mean = mean.reshape(PB * EDGE * EDGE, 256).astype(jnp.bfloat16)
    copy = np.zeros((4, 2, PB, 2, PB, 2, 4, PB, PB), np.float32)
    for q in range(4):
        for big_x in range(PB):
            for big_y in range(PB):
                copy[q, :, big_x, :, big_y, 0, q, big_x, big_y] = 1.0
    copy = copy.reshape(256, 128).astype(jnp.bfloat16)
    return plane, plane_rest, ghost, face, mean, copy


def dot(left, right):
    return lax.dot_general(
        left, right, (((1,), (0,)), ((), ())), preferred_element_type=F32
    )


def dot_t(left, right):
    return lax.dot_general(
        left, right, (((1,), (1,)), ((), ())), preferred_element_type=F32
    )


def split(values):
    high = values.astype(BF16)
    return high, (values - high.astype(F32)).astype(BF16)


def ring_field(coarse_ref, number_ref, left_ref, right_ref, q, x):
    if x < 8:
        return coarse_ref[q, x] if q < 4 else number_ref[x]
    return right_ref[q, x - 8] if x < 12 else left_ref[q, x - 12]


def y_kernel(coarse_ref, number_ref, left_ref, right_ref, low_ref, high_ref):
    top = lax.broadcasted_iota(jnp.int32, (8, 128), 0) < 4
    field = functools.partial(ring_field, coarse_ref, number_ref, left_ref, right_ref)
    for q in range(5):
        for pair in range(8):
            even, odd = field(q, 2 * pair), field(q, 2 * pair + 1)
            at = pl.ds((q * 8 + pair) * 8, 8)
            low_ref[at] = jnp.where(top, even, pltpu.roll(odd, 4, 0))
            high_ref[at] = jnp.where(top, pltpu.roll(even, 4, 0), odd)


def z_kernel(
    coarse_ref, number_ref, left_ref, right_ref, below_ref, above_ref, all_ref, low_ref, high_ref
):
    top = lax.broadcasted_iota(jnp.int32, (8, 128), 0) < 4
    field = functools.partial(ring_field, coarse_ref, number_ref, left_ref, right_ref)
    for q in range(5):
        for pair in range(8):
            at = pl.ds((q * 8 + pair) * 8, 8)
            below, above = below_ref[at], above_ref[at]
            row = (q * 16 + 2 * pair) * 16
            all_ref[pl.ds(row, 8)] = field(q, 2 * pair)
            all_ref[pl.ds(row + 8, 8)] = jnp.where(top, above, pltpu.roll(below, 4, 0))
            all_ref[pl.ds(row + 16, 8)] = field(q, 2 * pair + 1)
            all_ref[pl.ds(row + 24, 8)] = jnp.where(top, pltpu.roll(above, 4, 0), below)
    group = lax.broadcasted_iota(jnp.int32, (40, 128), 1) // 4
    low = jnp.zeros((40, 128), F32)
    high = jnp.zeros((40, 128), F32)
    for g in range(32):
        rows = all_ref[pl.ds(g * 40, 40)]
        low = jnp.where(group == g, pltpu.roll(rows, 4 * g, 1) if g else rows, low)
        shift = (4 * g + 4) % 128
        high = jnp.where(group == g, pltpu.roll(rows, shift, 1) if shift else rows, high)
    low_ref[...] = low
    high_ref[...] = high


def rate_parts(center, x_near, x_far, y_axis, wind):
    rows, lanes = center.shape
    y_up, y_down = pltpu.roll(center, rows - 1, y_axis), pltpu.roll(center, 1, y_axis)
    y_up2, y_down2 = pltpu.roll(center, rows - 2, y_axis), pltpu.roll(center, 2, y_axis)
    z_up, z_down = pltpu.roll(center, lanes - 1, 1), pltpu.roll(center, 1, 1)
    z_up2, z_down2 = pltpu.roll(center, lanes - 2, 1), pltpu.roll(center, 2, 1)
    laplace = (
        (x_near[0] + x_near[1]) + (y_up + y_down) + (z_up + z_down) - 6.0 * center
    )
    advect = (
        (wind[0] / 12.0) * (8.0 * (x_near[0] - x_near[1]) - (x_far[0] - x_far[1]))
        + (wind[1] / 12.0) * (8.0 * (y_up - y_down) - (y_up2 - y_down2))
        + (wind[2] / 12.0) * (8.0 * (z_up - z_down) - (z_up2 - z_down2))
    )
    return laplace, advect


HALF_PLACES = tuple(range(10)) + (14, 15)
WINDOW_PLACES = (14, 15) + tuple(range(10))


def half_kernel(
    all_ref, before_ref, after_ref, cells_ref, number_ref, mean_ref, pay_ref, half_ref, now_ref, cut_ref
):
    lane40 = lax.broadcasted_iota(jnp.int32, (40, 128), 1)
    before, after = before_ref[...], after_ref[...]
    for g in range(32):
        ahead = pltpu.roll(after, (128 - 4 * g) % 128, 1) if g else after
        shift = (124 - 4 * g) % 128
        behind = pltpu.roll(before, shift, 1) if shift else before
        rows = pl.ds(g * 40, 40)
        now_ref[rows, pl.ds(0, 128)] = all_ref[rows]
        now_ref[rows, pl.ds(128, 128)] = jnp.where(
            lane40 < 4, ahead, jnp.where(lane40 >= 124, behind, 0.0)
        )

    def sheet(q, x):
        return now_ref[pl.ds((q * 16 + x) * 16, 16)]

    for x in HALF_PLACES:
        number = sheet(4, x)
        for q in range(4):
            center = sheet(q, x)
            near = (sheet(q, (x + 1) % 16), sheet(q, (x - 1) % 16))
            far = (sheet(q, (x + 2) % 16), sheet(q, (x - 2) % 16))
            laplace, advect = rate_parts(center, near, far, 0, WIND_COARSE)
            stepped = center + number * laplace - advect
            half_ref[pl.ds((q * 16 + x) * 16, 16)] = jnp.where(number > 0.0, stepped, 0.0)

    cells = cells_ref[pl.ds(0, 1), pl.ds(0, 128)]
    lane = lax.broadcasted_iota(jnp.int32, (1, 128), 1)
    wanted = (4 * (cells & 31) - 2 + (lane & 7)) & 255
    place = lax.broadcasted_iota(jnp.int32, (256, 128), 0)
    pick = jnp.where((place == wanted) & (cells >= 0), 1.0, 0.0).astype(BF16)
    far_x = jnp.broadcast_to(((cells >> 6) & 1) == 1, (16, 128))
    far_y = jnp.broadcast_to(((cells >> 5) & 1) == 1, (8, 128))
    for t, field_ref in enumerate((now_ref, half_ref)):
        for q in range(4):
            cut = []
            for first, count in ((14, 2), (0, 10)):
                high, low = split(field_ref[pl.ds((q * 16 + first) * 16, count * 16)])
                cut.append(dot(high, pick) + dot(low, pick))
            cut = jnp.concatenate(cut, axis=0)
            for i in range(8):
                rows = jnp.where(
                    far_x, cut[(i + 4) * 16 : (i + 5) * 16], cut[i * 16 : (i + 1) * 16]
                )
                near_rows = pltpu.roll(rows, 2, 0)[:8]
                far_rows = pltpu.roll(rows, 14, 0)[:8]
                cut_ref[pl.ds(((t * 4 + q) * 8 + i) * 8, 8)] = jnp.where(
                    far_y, far_rows, near_rows
                )
    group = lax.broadcasted_iota(jnp.int32, (32, 128), 1) // 8
    pieces = [
        cut_ref[pl.ds(t * 256 + y, 32, stride=8)] for t in range(2) for y in range(8)
    ]
    for step in (8, 4, 2, 1):
        swap = (group & step) != 0
        for i in range(16):
            if not i & step:
                a, b = pieces[i], pieces[i + step]
                pieces[i] = jnp.where(swap, pltpu.roll(b, 8 * step, 1), a)
                pieces[i + step] = jnp.where(swap, b, pltpu.roll(a, 128 - 8 * step, 1))
    for slot in range(HOSTS):
        pay_ref[pl.ds(slot * SLOT_ROWS, 32)] = pieces[slot]
    for column in range(32):
        pay_ref[pl.ds(NUMBER_ROW + column, HOSTS, stride=SLOT_ROWS)] = number_ref[
            :, pl.ds(column * 128, 128)
        ]
    for side in range(2):
        pay_ref[pl.ds(MEAN_ROW + side, HOSTS, stride=SLOT_ROWS)] = mean_ref[
            :, pl.ds(side * 128, 128)
        ]
    placed = cells_ref[pl.ds(16, HOSTS), pl.ds(0, 128)] >= 0
    pay_ref[pl.ds(FLAG_ROW, HOSTS, stride=SLOT_ROWS)] = jnp.where(placed, 1.0, 0.0)


def full_kernel(coarse_ref, number_ref, half_ref, cells_ref, full_ref):
    lane = lax.broadcasted_iota(jnp.int32, (HOSTS, 128), 1)
    top = lax.broadcasted_iota(jnp.int32, (8, 128), 0) < 4
    cells = cells_ref[pl.ds(16, HOSTS), pl.ds(0, 128)]
    hit = (lane >> 2) == (cells & 31)
    covered = [
        jnp.max(jnp.where(hit & ((cells >> 5) == corner), 1, 0), axis=0, keepdims=True)
        for corner in range(4)
    ]

    def sheet(q, x):
        return half_ref[pl.ds((q * 16 + x % 16) * 16, 16)]

    for x in range(8):
        keep = jnp.where(top, covered[(x // 4) * 2], covered[(x // 4) * 2 + 1]) == 0
        number = number_ref[x]
        for q in range(4):
            center = sheet(q, x)
            laplace, advect = rate_parts(
                center,
                (sheet(q, x + 1), sheet(q, x - 1)),
                (sheet(q, x + 2), sheet(q, x - 2)),
                0,
                WIND_COARSE,
            )
            done = 0.5 * (
                coarse_ref[q, x]
                + center[:8, :128]
                + number * laplace[:8, :128]
                - advect[:8, :128]
            )
            full_ref[q, x] = jnp.where(keep, done, 0.0)


def put_means(back, full_ref, cells_ref, copy_ref, next_ref):
    even, odd = back[:, :128], back[:, 128:]
    values = jnp.concatenate(
        [even, pltpu.roll(even, 64, 1), odd, pltpu.roll(odd, 64, 1)], axis=0
    )
    high = values.astype(BF16)
    low, lowest = split(values - high.astype(F32))
    parts = jnp.concatenate([high, low, lowest, jnp.zeros_like(high)], axis=0)
    spread = dot_t(copy_ref[...], parts)
    cells = cells_ref[pl.ds(8, 1)]
    row = lax.broadcasted_iota(jnp.int32, (256, 1), 0)
    corner = ((row >> 5) & 1) * 2 + ((row >> 2) & 1)
    spread = jnp.where((cells >> 5) == corner, spread, 0.0).astype(BF16)
    z = lax.broadcasted_iota(jnp.int32, (128, 256), 0)
    lane = lax.broadcasted_iota(jnp.int32, (128, 256), 1)
    here = ((z >> 2) == (cells & 31)) & ((z & 3) == ((lane >> 4) & 3)) & (cells >= 0)
    added = dot_t(spread, jnp.where(here, 1.0, 0.0).astype(BF16))
    for q in range(4):
        for x in range(8):
            at = (q * 8 + x) * 8
            next_ref[q, x] = full_ref[q, x] + added[at : at + 8]


def plane_parts(field, plane_ref, rest_ref):
    high, low = split(field)
    both = dot(high, plane_ref[pl.ds(0, 256)]) + dot(low, plane_ref[pl.ds(256, 256)])
    return both[:, :256], both[:, 256:] + dot(high, rest_ref[...])


def plus(left, right):
    if left is None or right is None:
        return right if left is None else left
    return left + right


def minus(left, right):
    if right is None:
        return left
    return -right if left is None else left - right


def x_parts(padded):
    laplace, advect = [], []
    for x in range(2, 18):
        near = minus(padded[x + 1], padded[x - 1])
        far = minus(padded[x + 2], padded[x - 2])
        laplace.append(plus(padded[x + 1], padded[x - 1]))
        near = None if near is None else (8.0 * WIND_FINE[0] / 12.0) * near
        far = None if far is None else (WIND_FINE[0] / 12.0) * far
        advect.append(minus(near, far))
    return laplace, advect


def plane(values, x):
    return values[x * HOSTS : (x + 1) * HOSTS]


def rate_of(numbers, padded, laplace, advect):
    x_laplace, x_advect = x_parts(padded)
    return [
        numbers[x] * plus(x_laplace[x], plane(laplace, x)) - plus(x_advect[x], plane(advect, x))
        for x in range(EDGE)
    ]


def means(planes, mean_ref):
    total = None
    for big_x in range(PB):
        group = planes[big_x * 4 : big_x * 4 + 4]
        high, low = split((group[0] + group[1]) + (group[2] + group[3]))
        weights = mean_ref[pl.ds(big_x * 256, 256)]
        total = plus(total, dot(high, weights) + dot(low, weights))
    return total


def lane_of_q():
    return (lax.broadcasted_iota(jnp.int32, (HOSTS, 256), 1) >> 4) & 3


def early_kernel(fine_ref, number_ref, plane_ref, rest_ref, mean_ref, route_ref, step_ref, back_ref, cells_ref):
    numbers = [number_ref[:, pl.ds(x * 256, 256)] for x in range(EDGE)]
    nothing = [None, None]
    back = jnp.zeros((HOSTS, 256), F32)
    for q in range(4):
        planes = []
        for x in range(EDGE):
            sides = [
                fine_ref[pl.ds((2 * x + side) * 4 + q, HOSTS, stride=128)] for side in range(2)
            ]
            planes.append(jnp.concatenate(sides, axis=1))
        parts = plane_parts(jnp.concatenate(planes, axis=0), plane_ref, rest_ref)
        rate = rate_of(numbers, nothing + planes + nothing, *parts)
        half = [planes[x] + rate[x] for x in range(EDGE)]
        parts = plane_parts(jnp.concatenate(half, axis=0), plane_ref, rest_ref)
        rate = rate_of(numbers, nothing + half + nothing, *parts)
        done = [0.5 * (planes[x] + half[x] + rate[x]) for x in range(EDGE)]
        for x in range(EDGE):
            step_ref[pl.ds((q * EDGE + x) * HOSTS, HOSTS)] = done[x]
        back = jnp.where(lane_of_q() == q, means(done, mean_ref), back)
    back_ref[...] = back
    lane = lax.broadcasted_iota(jnp.int32, (8, 256), 1)
    row = lax.broadcasted_iota(jnp.int32, (HOSTS, 256), 0)
    by_eight = jnp.zeros((8, 256), jnp.int32)
    by_one = jnp.zeros((8, 256), jnp.int32)
    by_row = jnp.zeros((HOSTS, 256), jnp.int32)
    for slot in range(HOSTS):
        cell = route_ref[slot]
        by_eight = jnp.where(((lane >> 3) & 15) == slot, cell, by_eight)
        by_one = jnp.where((lane & 15) == slot, cell, by_one)
        by_row = jnp.where(row == slot, cell, by_row)
    cells_ref[pl.ds(0, 8)] = by_eight
    cells_ref[pl.ds(8, 8)] = by_one
    cells_ref[pl.ds(16, HOSTS)] = by_row


def ghosts(block_ref, q, t, ghost_ref, face_ref):
    interp = interp_table(PB, RATIO)
    first_half = lax.broadcasted_iota(jnp.int32, (HOSTS, 128), 1) < 64
    coarse = []
    for x in range(8):
        rows = block_ref[pl.ds(q * 8 + x, HOSTS, stride=SLOT_ROWS)]
        turned = pltpu.roll(rows, 64, 1)
        coarse.append(
            jnp.where(first_half, rows, turned) if t == 0 else jnp.where(first_half, turned, rows)
        )
    inner, outer = [], []
    for i in range(EDGE + 4):
        total = None
        for j in range(8):
            if interp[i, j] != 0.0:
                total = plus(total, float(interp[i, j]) * coarse[j])
        (inner if 2 <= i < EDGE + 2 else outer).append(total)
    sides = dot(jnp.concatenate(split(jnp.concatenate(inner, axis=0)), axis=1), ghost_ref[...])
    faces = dot(jnp.concatenate(split(jnp.concatenate(outer, axis=0)), axis=1), face_ref[...])
    return sides[:, :256], sides[:, 256:], [plane(faces, i) for i in range(4)]


def ghost_part(block_ref, numbers, q, plane_ref, rest_ref, ghost_ref, face_ref):
    laplace, advect, faces = ghosts(block_ref, q, 0, ghost_ref, face_ref)
    half = rate_of(numbers, faces[:2] + [None] * EDGE + faces[2:], laplace, advect)
    laplace, advect, faces = ghosts(block_ref, q, 1, ghost_ref, face_ref)
    parts = plane_parts(jnp.concatenate(half, axis=0), plane_ref, rest_ref)
    rate = rate_of(
        numbers, faces[:2] + half + faces[2:], parts[0] + laplace, parts[1] + advect
    )
    return [0.5 * (half[x] + rate[x]) for x in range(EDGE)]


def late_kernel(
    block_ref, step_ref, old_ref, number_ref, plane_ref, rest_ref, ghost_ref, face_ref, fine_ref
):
    numbers = [number_ref[:, pl.ds(x * 256, 256)] for x in range(EDGE)]
    placed = block_ref[pl.ds(FLAG_ROW, HOSTS, stride=SLOT_ROWS)] > 0.5
    for q in range(4):
        added = ghost_part(block_ref, numbers, q, plane_ref, rest_ref, ghost_ref, face_ref)
        for x in range(EDGE):
            done = step_ref[pl.ds((q * EDGE + x) * HOSTS, HOSTS)] + added[x]
            for side in range(2):
                at = pl.ds((2 * x + side) * 4 + q, HOSTS, stride=128)
                fine_ref[at] = jnp.where(
                    placed, done[:, side * 128 : side * 128 + 128], old_ref[at]
                )


def back_kernel(
    sent_ref,
    got_ref,
    full_ref,
    cells_ref,
    copy_ref,
    plane_ref,
    rest_ref,
    ghost_ref,
    face_ref,
    mean_ref,
    next_ref,
):
    def got(row):
        sides = [got_ref[pl.ds(row + side, HOSTS, stride=SLOT_ROWS)] for side in range(2)]
        return jnp.concatenate(sides, axis=1)

    numbers = [got(NUMBER_ROW + 2 * x) for x in range(EDGE)]
    back = jnp.zeros((HOSTS, 256), F32)
    for q in range(4):
        added = ghost_part(sent_ref, numbers, q, plane_ref, rest_ref, ghost_ref, face_ref)
        back = jnp.where(lane_of_q() == q, means(added, mean_ref), back)
    put_means(back + got(MEAN_ROW), full_ref, cells_ref, copy_ref, next_ref)


def call(kernel, operands, outs, smem=(), scratch=(), flops=1000000, name=None):
    vmem = pl.BlockSpec(memory_space=pltpu.VMEM)
    scalar = pl.BlockSpec(memory_space=pltpu.SMEM)
    moved = sum(int(np.prod(o.shape)) * o.dtype.itemsize for o in operands)
    return pl.pallas_call(
        kernel,
        out_shape=tuple(jax.ShapeDtypeStruct(shape, dtype) for shape, dtype in outs),
        in_specs=[scalar if i in smem else vmem for i in range(len(operands))],
        out_specs=tuple(vmem for _ in outs),
        scratch_shapes=[pltpu.VMEM(shape, F32) for shape in scratch],
        compiler_params=pltpu.CompilerParams(vmem_limit_bytes=LIMIT * 1024 * 1024),
        cost_estimate=pl.CostEstimate(flops=flops, bytes_accessed=moved, transcendentals=0),
        name=name,
    )(*operands)


def shards(coarse_state, diffusion_number, route_cell, fine_state, fine_diffusion):
    flat, rest, ghost, face, mean, copy = (jnp.asarray(table) for table in tables())
    fine_rows = fine_state.reshape(HOSTS, 4, 32, 128).transpose(0, 2, 1, 3).reshape(2048, 128)
    fine_numbers = fine_diffusion.reshape(HOSTS, EDGE**3)

    def exchange(low, high, axis, up_first):
        count = lax.axis_size(axis)
        up = [(i, i + 1) for i in range(count - 1)]
        down = [(i + 1, i) for i in range(count - 1)]
        if up_first:
            from_below = lax.ppermute(high, axis, up)
            return from_below, lax.ppermute(low, axis, down)
        from_above = lax.ppermute(low, axis, down)
        return lax.ppermute(high, axis, up), from_above

    fields = jnp.concatenate([coarse_state, diffusion_number[None]], axis=0)
    left, right = exchange(fields[:, :4], fields[:, 4:], "gx", True)
    own = (coarse_state, diffusion_number, left, right)
    low, high = call(y_kernel, own, [((320, 128), F32)] * 2, name="y_messages")
    below, above = exchange(low, high, "gy", True)
    everything, low, high = call(
        z_kernel,
        own + (below, above),
        [((1280, 128), F32), ((40, 128), F32), ((40, 128), F32)],
        name="z_messages",
    )
    before, after = exchange(low, high, "gz", False)
    step, early_means, cells = call(
        early_kernel,
        (fine_rows, fine_numbers, flat, rest, mean, route_cell.reshape(HOSTS)),
        [((1024, 256), F32), ((HOSTS, 256), F32), ((32, 256), jnp.int32)],
        smem=(5,),
        flops=10**9,
        name="fine_early",
    )
    sent, half = call(
        half_kernel,
        (everything, before, after, cells, fine_numbers, early_means),
        [((HOSTS * SLOT_ROWS, 128), F32), ((1024, 256), F32)],
        scratch=[(1280, 256), (512, 128)],
        name="half_step",
    )
    got = lax.all_to_all(
        sent.reshape(HOSTS, SLOT_ROWS, 1, 128), "gz", split_axis=0, concat_axis=0, tiled=True
    ).reshape(HOSTS * SLOT_ROWS, 128)
    (full,) = call(
        full_kernel,
        (coarse_state, diffusion_number, half, cells),
        [((4, 8, 8, 128), F32)],
        name="coarse_full",
    )
    (coarse_next,) = call(
        back_kernel,
        (sent, got, full, cells, copy, flat, rest, ghost, face, mean),
        [((4, 8, 8, 128), F32)],
        flops=10**9,
        name="coarse_next",
    )
    (fine_done,) = call(
        late_kernel,
        (got, step, fine_rows, fine_numbers, flat, rest, ghost, face),
        [((2048, 128), F32)],
        flops=10**9,
        name="fine_next",
    )
    fine_next = (
        fine_done.reshape(HOSTS, 32, 4, 128).transpose(0, 2, 1, 3).reshape(fine_state.shape)
    )
    return coarse_next, fine_next


def solution(mesh):
    return jax.shard_map(
        shards,
        mesh=mesh,
        in_specs=(
            P(None, "gx", "gy", "gz"),
            P("gx", "gy", "gz"),
            P("gx", "gy", "gz", None),
            P("gx", "gy", "gz", None, None, None),
            P("gx", "gy", "gz", None, None),
        ),
        out_specs=(P(None, "gx", "gy", "gz"), P("gx", "gy", "gz", None, None, None)),
        check_vma=False,
    )
```

```python
import functools
import math

import jax
import jax.numpy as jnp
import numpy as np
from jax import lax
from jax.experimental import pallas as pl
from jax.experimental.pallas import tpu as pltpu
from jax.sharding import PartitionSpec as P

PB = 4
RATIO = 4
EDGE = PB * RATIO
HOSTS = 16
LIMIT = 16
NUMBER_ROW = 32
MEAN_ROW = 64
FLAG_ROW = 66
SLOT_ROWS = 67
WIND_COARSE = (0.05, 0.03, 0.07)
WIND_FINE = tuple(RATIO * speed for speed in WIND_COARSE)
F32 = jnp.float32
BF16 = jnp.bfloat16


def interp_table(coarse_count, ratio):
    fine_total = coarse_count * ratio + 4
    weights_table = np.zeros((fine_total, coarse_count + 4), np.float32)
    for fine_index in range(fine_total):
        position = (fine_index - 1.5) / ratio + 2.0
        first_node = math.floor(position - 0.5) - 1
        for offset in range(4):
            weight = 1.0
            for other_node in range(4):
                if other_node != offset:
                    weight = (
                        weight
                        * (position - (first_node + other_node + 0.5))
                        / (offset - other_node)
                    )
            weights_table[fine_index, first_node + offset] = weight
    return weights_table


def high_low(table):
    high = np.asarray(table, np.float32).astype(jnp.bfloat16)
    low = (np.asarray(table, np.float64) - high.astype(np.float64)).astype(jnp.bfloat16)
    return high, low


def tables():
    interp = interp_table(PB, RATIO).astype(np.float64)
    span = EDGE + 4
    lap = np.zeros((span, span, EDGE * EDGE))
    adv = np.zeros((span, span, EDGE * EDGE))
    for y in range(EDGE):
        for z in range(EDGE):
            col = y * EDGE + z
            lap[y + 2, z + 2, col] = -6.0
            for dy, dz, wind in ((1, 0, WIND_FINE[1]), (0, 1, WIND_FINE[2])):
                for sign in (1, -1):
                    lap[y + 2 + sign * dy, z + 2 + sign * dz, col] += 1.0
                    adv[y + 2 + sign * dy, z + 2 + sign * dz, col] += sign * 8.0 * wind / 12.0
                    adv[y + 2 + sign * 2 * dy, z + 2 + sign * 2 * dz, col] -= sign * wind / 12.0
    inner = np.zeros((span, span), bool)
    inner[2:-2, 2:-2] = True
    inner = inner.reshape(-1)
    both = np.concatenate([lap.reshape(span * span, -1), adv.reshape(span * span, -1)], axis=1)
    plane_hi, plane_lo = high_low(both[inner])
    spread = np.kron(interp, interp)
    ghost_hi, ghost_lo = high_low(spread.T @ np.where(inner[:, None], 0.0, both))
    face_hi, face_lo = high_low(spread[inner].T)
    mean = np.zeros((EDGE, EDGE, PB, 4, PB, PB), np.float32)
    for y in range(EDGE):
        for z in range(EDGE):
            mean[y, z, z // RATIO, :, :, y // RATIO] = 1.0 / RATIO**3
    copy = np.zeros((4, 2, PB, 2, PB, 2, 4, PB, PB), np.float32)
    for q in range(4):
        for big_x in range(PB):
            for big_y in range(PB):
                copy[q, :, big_x, :, big_y, 0, q, big_x, big_y] = 1.0
    table = np.zeros((4, 256, 512), jnp.bfloat16)
    table[0] = plane_hi
    table[1] = np.concatenate([ghost_hi, ghost_lo, ghost_hi, np.zeros_like(ghost_hi)], axis=0)
    table[2, :, :256] = plane_lo[:, 256:]
    table[2, :, 256:] = np.concatenate([face_hi, face_lo, face_hi, np.zeros_like(face_hi)], axis=0)
    table[3, :, :256] = mean.reshape(256, 256)
    table[3, :, 256:384] = copy.reshape(256, 128)
    return table.reshape(1024, 512)


PLANE = (pl.ds(0, 256), pl.ds(0, 512))
GHOST = (pl.ds(256, 256), pl.ds(0, 512))
REST = (pl.ds(512, 256), pl.ds(0, 256))
FACE = (pl.ds(512, 256), pl.ds(256, 256))
MEAN = (pl.ds(768, 256), pl.ds(0, 256))
COPY = (pl.ds(768, 256), pl.ds(256, 128))


def dot(left, right):
    return lax.dot_general(
        left, right, (((1,), (0,)), ((), ())), preferred_element_type=F32
    )


def dot_t(left, right):
    return lax.dot_general(
        left, right, (((1,), (1,)), ((), ())), preferred_element_type=F32
    )


def split(values):
    high = values.astype(BF16)
    return high, (values - high.astype(F32)).astype(BF16)


def ring_field(first_ref, last_ref, left_ref, right_ref, q, x):
    return (first_ref, last_ref, right_ref, left_ref)[x // 4][q, x % 4]


def y_kernel(first_ref, last_ref, left_ref, right_ref, low_ref, high_ref):
    top = lax.broadcasted_iota(jnp.int32, (8, 128), 0) < 4
    field = functools.partial(ring_field, first_ref, last_ref, left_ref, right_ref)
    for q in range(5):
        for pair in range(8):
            even, odd = field(q, 2 * pair), field(q, 2 * pair + 1)
            at = pl.ds((q * 8 + pair) * 8, 8)
            low_ref[at] = jnp.where(top, even, pltpu.roll(odd, 4, 0))
            high_ref[at] = jnp.where(top, pltpu.roll(even, 4, 0), odd)


def z_kernel(
    first_ref, last_ref, left_ref, right_ref, below_ref, above_ref, all_ref, low_ref, high_ref
):
    top = lax.broadcasted_iota(jnp.int32, (8, 128), 0) < 4
    field = functools.partial(ring_field, first_ref, last_ref, left_ref, right_ref)
    for q in range(5):
        for pair in range(8):
            at = pl.ds((q * 8 + pair) * 8, 8)
            below, above = below_ref[at], above_ref[at]
            row = (q * 16 + 2 * pair) * 16
            all_ref[pl.ds(row, 8)] = field(q, 2 * pair)
            all_ref[pl.ds(row + 8, 8)] = jnp.where(top, above, pltpu.roll(below, 4, 0))
            all_ref[pl.ds(row + 16, 8)] = field(q, 2 * pair + 1)
            all_ref[pl.ds(row + 24, 8)] = jnp.where(top, pltpu.roll(above, 4, 0), below)
    group = lax.broadcasted_iota(jnp.int32, (40, 128), 1) // 4
    low = jnp.zeros((40, 128), F32)
    high = jnp.zeros((40, 128), F32)
    for g in range(32):
        rows = all_ref[pl.ds(g * 40, 40)]
        low = jnp.where(group == g, pltpu.roll(rows, 4 * g, 1) if g else rows, low)
        shift = (4 * g + 4) % 128
        high = jnp.where(group == g, pltpu.roll(rows, shift, 1) if shift else rows, high)
    low_ref[...] = low
    high_ref[...] = high


def rate_parts(center, x_near, x_far, y_axis, wind):
    rows, lanes = center.shape
    y_up, y_down = pltpu.roll(center, rows - 1, y_axis), pltpu.roll(center, 1, y_axis)
    y_up2, y_down2 = pltpu.roll(center, rows - 2, y_axis), pltpu.roll(center, 2, y_axis)
    z_up, z_down = pltpu.roll(center, lanes - 1, 1), pltpu.roll(center, 1, 1)
    z_up2, z_down2 = pltpu.roll(center, lanes - 2, 1), pltpu.roll(center, 2, 1)
    laplace = (
        (x_near[0] + x_near[1]) + (y_up + y_down) + (z_up + z_down) - 6.0 * center
    )
    advect = (
        (wind[0] / 12.0) * (8.0 * (x_near[0] - x_near[1]) - (x_far[0] - x_far[1]))
        + (wind[1] / 12.0) * (8.0 * (y_up - y_down) - (y_up2 - y_down2))
        + (wind[2] / 12.0) * (8.0 * (z_up - z_down) - (z_up2 - z_down2))
    )
    return laplace, advect


HALF_PLACES = tuple(range(10)) + (14, 15)
WINDOW_PLACES = (14, 15) + tuple(range(10))


def half_kernel(
    all_ref,
    before_ref,
    after_ref,
    cells_ref,
    number_ref,
    mean_ref,
    sent_ref,
    full_ref,
    now_ref,
    half_ref,
    cut_ref,
    pay_ref,
    sem,
):
    lane40 = lax.broadcasted_iota(jnp.int32, (40, 128), 1)
    before, after = before_ref[...], after_ref[...]
    for g in range(32):
        ahead = pltpu.roll(after, (128 - 4 * g) % 128, 1) if g else after
        shift = (124 - 4 * g) % 128
        behind = pltpu.roll(before, shift, 1) if shift else before
        rows = pl.ds(g * 40, 40)
        now_ref[rows, pl.ds(0, 128)] = all_ref[rows]
        now_ref[rows, pl.ds(128, 128)] = jnp.where(
            lane40 < 4, ahead, jnp.where(lane40 >= 124, behind, 0.0)
        )

    def sheet(q, x):
        return now_ref[pl.ds((q * 16 + x) * 16, 16)]

    for x in HALF_PLACES:
        number = sheet(4, x)
        for q in range(4):
            center = sheet(q, x)
            near = (sheet(q, (x + 1) % 16), sheet(q, (x - 1) % 16))
            far = (sheet(q, (x + 2) % 16), sheet(q, (x - 2) % 16))
            laplace, advect = rate_parts(center, near, far, 0, WIND_COARSE)
            stepped = center + number * laplace - advect
            half_ref[pl.ds((q * 16 + x) * 16, 16)] = jnp.where(number > 0.0, stepped, 0.0)

    cells = cells_ref[pl.ds(0, 1), pl.ds(0, 128)]
    lane = lax.broadcasted_iota(jnp.int32, (1, 128), 1)
    wanted = (4 * (cells & 31) - 2 + (lane & 7)) & 255
    place = lax.broadcasted_iota(jnp.int32, (256, 128), 0)
    pick = jnp.where((place == wanted) & (cells >= 0), 1.0, 0.0).astype(BF16)
    far_x = jnp.broadcast_to(((cells >> 6) & 1) == 1, (16, 128))
    far_y = jnp.broadcast_to(((cells >> 5) & 1) == 1, (8, 128))
    for t, field_ref in enumerate((now_ref, half_ref)):
        for q in range(4):
            cut = []
            for first, count in ((14, 2), (0, 10)):
                high, low = split(field_ref[pl.ds((q * 16 + first) * 16, count * 16)])
                cut.append(dot(high, pick) + dot(low, pick))
            cut = jnp.concatenate(cut, axis=0)
            for i in range(8):
                rows = jnp.where(
                    far_x, cut[(i + 4) * 16 : (i + 5) * 16], cut[i * 16 : (i + 1) * 16]
                )
                near_rows = pltpu.roll(rows, 2, 0)[:8]
                far_rows = pltpu.roll(rows, 14, 0)[:8]
                cut_ref[pl.ds(((t * 4 + q) * 8 + i) * 8, 8)] = jnp.where(
                    far_y, far_rows, near_rows
                )
    group = lax.broadcasted_iota(jnp.int32, (32, 128), 1) // 8
    pieces = [
        cut_ref[pl.ds(t * 256 + y, 32, stride=8)] for t in range(2) for y in range(8)
    ]
    for step in (8, 4, 2, 1):
        swap = (group & step) != 0
        for i in range(16):
            if not i & step:
                a, b = pieces[i], pieces[i + step]
                pieces[i] = jnp.where(swap, pltpu.roll(b, 8 * step, 1), a)
                pieces[i + step] = jnp.where(swap, b, pltpu.roll(a, 128 - 8 * step, 1))
    for slot in range(HOSTS):
        pay_ref[pl.ds(slot * SLOT_ROWS, 32)] = pieces[slot]
    for column in range(32):
        pay_ref[pl.ds(NUMBER_ROW + column, HOSTS, stride=SLOT_ROWS)] = number_ref[
            :, pl.ds(column * 128, 128)
        ]
    for side in range(2):
        pay_ref[pl.ds(MEAN_ROW + side, HOSTS, stride=SLOT_ROWS)] = mean_ref[
            :, pl.ds(side * 128, 128)
        ]
    placed = cells_ref[pl.ds(16, HOSTS), pl.ds(0, 128)] >= 0
    pay_ref[pl.ds(FLAG_ROW, HOSTS, stride=SLOT_ROWS)] = jnp.where(placed, 1.0, 0.0)
    copy = pltpu.make_async_copy(pay_ref, sent_ref, sem)
    copy.start()
    full_step(now_ref, half_ref, cells_ref, full_ref)
    copy.wait()


def full_step(now_ref, half_ref, cells_ref, full_ref):
    lane = lax.broadcasted_iota(jnp.int32, (HOSTS, 128), 1)
    top = lax.broadcasted_iota(jnp.int32, (8, 128), 0) < 4
    cells = cells_ref[pl.ds(16, HOSTS), pl.ds(0, 128)]
    hit = (lane >> 2) == (cells & 31)
    covered = [
        jnp.max(jnp.where(hit & ((cells >> 5) == corner), 1, 0), axis=0, keepdims=True)
        for corner in range(4)
    ]

    def sheet(q, x):
        return half_ref[pl.ds((q * 16 + x % 16) * 16, 16)]

    for x in range(8):
        keep = jnp.where(top, covered[(x // 4) * 2], covered[(x // 4) * 2 + 1]) == 0
        number = now_ref[pl.ds((64 + x) * 16, 8), pl.ds(0, 128)]
        for q in range(4):
            center = sheet(q, x)
            laplace, advect = rate_parts(
                center,
                (sheet(q, x + 1), sheet(q, x - 1)),
                (sheet(q, x + 2), sheet(q, x - 2)),
                0,
                WIND_COARSE,
            )
            done = 0.5 * (
                now_ref[pl.ds((q * 16 + x) * 16, 8), pl.ds(0, 128)]
                + center[:8, :128]
                + number * laplace[:8, :128]
                - advect[:8, :128]
            )
            full_ref[q, x] = jnp.where(keep, done, 0.0)


def put_means(back, full_ref, cells_ref, table_ref, next_ref):
    even, odd = back[:, :128], back[:, 128:]
    values = jnp.concatenate(
        [even, pltpu.roll(even, 64, 1), odd, pltpu.roll(odd, 64, 1)], axis=0
    )
    high = values.astype(BF16)
    low, lowest = split(values - high.astype(F32))
    parts = jnp.concatenate([high, low, lowest, jnp.zeros_like(high)], axis=0)
    spread = dot_t(table_ref[COPY], parts)
    cells = cells_ref[pl.ds(8, 1)]
    row = lax.broadcasted_iota(jnp.int32, (256, 1), 0)
    corner = ((row >> 5) & 1) * 2 + ((row >> 2) & 1)
    spread = jnp.where((cells >> 5) == corner, spread, 0.0).astype(BF16)
    z = lax.broadcasted_iota(jnp.int32, (128, 256), 0)
    lane = lax.broadcasted_iota(jnp.int32, (128, 256), 1)
    here = ((z >> 2) == (cells & 31)) & ((z & 3) == ((lane >> 4) & 3)) & (cells >= 0)
    added = dot_t(spread, jnp.where(here, 1.0, 0.0).astype(BF16))
    for q in range(4):
        for x in range(8):
            at = (q * 8 + x) * 8
            next_ref[q, x] = full_ref[q, x] + added[at : at + 8]


def plane_parts(field, table_ref):
    high, low = split(field)
    both = dot(high, table_ref[PLANE]) + dot(low, table_ref[PLANE])
    return both[:, :256], both[:, 256:] + dot(high, table_ref[REST])


def plus(left, right):
    if left is None or right is None:
        return right if left is None else left
    return left + right


def minus(left, right):
    if right is None:
        return left
    return -right if left is None else left - right


def x_parts(padded):
    laplace, advect = [], []
    for x in range(2, 18):
        near = minus(padded[x + 1], padded[x - 1])
        far = minus(padded[x + 2], padded[x - 2])
        laplace.append(plus(padded[x + 1], padded[x - 1]))
        near = None if near is None else (8.0 * WIND_FINE[0] / 12.0) * near
        far = None if far is None else (WIND_FINE[0] / 12.0) * far
        advect.append(minus(near, far))
    return laplace, advect


def plane(values, x):
    return values[x * HOSTS : (x + 1) * HOSTS]


def rate_of(numbers, padded, laplace, advect):
    x_laplace, x_advect = x_parts(padded)
    return [
        numbers[x] * plus(x_laplace[x], plane(laplace, x)) - plus(x_advect[x], plane(advect, x))
        for x in range(EDGE)
    ]


def means(planes, table_ref):
    sums = []
    for big_x in range(PB):
        group = planes[big_x * 4 : big_x * 4 + 4]
        sums.append((group[0] + group[1]) + (group[2] + group[3]))
    high, low = split(jnp.concatenate(sums, axis=0))
    every = dot(high, table_ref[MEAN]) + dot(low, table_ref[MEAN])
    lane_x = (lax.broadcasted_iota(jnp.int32, (HOSTS, 256), 1) >> 2) & 3
    total = plane(every, 0)
    for big_x in range(1, PB):
        total = jnp.where(lane_x == big_x, plane(every, big_x), total)
    return total


def lane_of_q():
    return (lax.broadcasted_iota(jnp.int32, (HOSTS, 256), 1) >> 4) & 3


def early_kernel(fine_ref, number_ref, table_ref, route_ref, step_ref, back_ref, cells_ref):
    numbers = [number_ref[:, pl.ds(x * 256, 256)] for x in range(EDGE)]
    nothing = [None, None]
    back = jnp.zeros((HOSTS, 256), F32)
    for q in range(4):
        planes = []
        for x in range(EDGE):
            sides = [
                fine_ref[pl.ds((2 * x + side) * 4 + q, HOSTS, stride=128)] for side in range(2)
            ]
            planes.append(jnp.concatenate(sides, axis=1))
        parts = plane_parts(jnp.concatenate(planes, axis=0), table_ref)
        rate = rate_of(numbers, nothing + planes + nothing, *parts)
        half = [planes[x] + rate[x] for x in range(EDGE)]
        parts = plane_parts(jnp.concatenate(half, axis=0), table_ref)
        rate = rate_of(numbers, nothing + half + nothing, *parts)
        done = [0.5 * (planes[x] + half[x] + rate[x]) for x in range(EDGE)]
        for x in range(EDGE):
            step_ref[pl.ds((q * EDGE + x) * HOSTS, HOSTS)] = done[x]
        back = jnp.where(lane_of_q() == q, means(done, table_ref), back)
    back_ref[...] = back
    lane = lax.broadcasted_iota(jnp.int32, (8, 256), 1)
    row = lax.broadcasted_iota(jnp.int32, (HOSTS, 256), 0)
    by_eight = jnp.zeros((8, 256), jnp.int32)
    by_one = jnp.zeros((8, 256), jnp.int32)
    by_row = jnp.zeros((HOSTS, 256), jnp.int32)
    for slot in range(HOSTS):
        cell = route_ref[slot]
        by_eight = jnp.where(((lane >> 3) & 15) == slot, cell, by_eight)
        by_one = jnp.where((lane & 15) == slot, cell, by_one)
        by_row = jnp.where(row == slot, cell, by_row)
    cells_ref[pl.ds(0, 8)] = by_eight
    cells_ref[pl.ds(8, 8)] = by_one
    cells_ref[pl.ds(16, HOSTS)] = by_row


def ghosts(block_ref, q, t, table_ref):
    interp = interp_table(PB, RATIO)
    first_half = lax.broadcasted_iota(jnp.int32, (HOSTS, 128), 1) < 64
    coarse = []
    for x in range(8):
        rows = block_ref[pl.ds(q * 8 + x, HOSTS, stride=SLOT_ROWS)]
        turned = pltpu.roll(rows, 64, 1)
        coarse.append(
            jnp.where(first_half, rows, turned) if t == 0 else jnp.where(first_half, turned, rows)
        )
    inner, outer = [], []
    for i in range(EDGE + 4):
        total = None
        for j in range(8):
            if interp[i, j] != 0.0:
                total = plus(total, float(interp[i, j]) * coarse[j])
        (inner if 2 <= i < EDGE + 2 else outer).append(total)
    sides = dot(jnp.concatenate(split(jnp.concatenate(inner, axis=0)), axis=1), table_ref[GHOST])
    faces = dot(jnp.concatenate(split(jnp.concatenate(outer, axis=0)), axis=1), table_ref[FACE])
    return sides[:, :256], sides[:, 256:], [plane(faces, i) for i in range(4)]


def ghost_part(block_ref, numbers, q, table_ref):
    laplace, advect, faces = ghosts(block_ref, q, 0, table_ref)
    half = rate_of(numbers, faces[:2] + [None] * EDGE + faces[2:], laplace, advect)
    laplace, advect, faces = ghosts(block_ref, q, 1, table_ref)
    parts = plane_parts(jnp.concatenate(half, axis=0), table_ref)
    rate = rate_of(
        numbers, faces[:2] + half + faces[2:], parts[0] + laplace, parts[1] + advect
    )
    return [0.5 * (half[x] + rate[x]) for x in range(EDGE)]


def last_kernel(
    got_ref,
    sent_hbm,
    step_hbm,
    old_hbm,
    number_hbm,
    full_ref,
    cells_ref,
    table_ref,
    fine_hbm,
    next_ref,
    sent_ref,
    step_ref,
    old_ref,
    number_ref,
    fine_ref,
    sems,
):
    copies = [
        pltpu.make_async_copy(src, dst, sems.at[i])
        for i, (src, dst) in enumerate(
            (
                (number_hbm, number_ref),
                (step_hbm, step_ref),
                (old_hbm, old_ref),
                (sent_hbm, sent_ref),
            )
        )
    ]
    for copy in copies:
        copy.start()

    def got(row):
        sides = [got_ref[pl.ds(row + side, HOSTS, stride=SLOT_ROWS)] for side in range(2)]
        return jnp.concatenate(sides, axis=1)

    placed = got_ref[pl.ds(FLAG_ROW, HOSTS, stride=SLOT_ROWS)] > 0.5
    copies[0].wait()
    numbers = [number_ref[:, pl.ds(x * 256, 256)] for x in range(EDGE)]
    for q in range(4):
        added = ghost_part(got_ref, numbers, q, table_ref)
        if q == 0:
            copies[1].wait()
            copies[2].wait()
        for x in range(EDGE):
            done = step_ref[pl.ds((q * EDGE + x) * HOSTS, HOSTS)] + added[x]
            for side in range(2):
                at = pl.ds((2 * x + side) * 4 + q, HOSTS, stride=128)
                fine_ref[at] = jnp.where(
                    placed, done[:, side * 128 : side * 128 + 128], old_ref[at]
                )
    out = pltpu.make_async_copy(fine_ref, fine_hbm, sems.at[4])
    out.start()
    copies[3].wait()
    numbers = [got(NUMBER_ROW + 2 * x) for x in range(EDGE)]
    back = jnp.zeros((HOSTS, 256), F32)
    for q in range(4):
        added = ghost_part(sent_ref, numbers, q, table_ref)
        back = jnp.where(lane_of_q() == q, means(added, table_ref), back)
    put_means(back + got(MEAN_ROW), full_ref, cells_ref, table_ref, next_ref)
    out.wait()


def call(kernel, operands, outs, smem=(), hbm=(), hbm_outs=(), scratch=(), flops=10**6, name=None):
    vmem = pl.BlockSpec(memory_space=pltpu.VMEM)
    scalar = pl.BlockSpec(memory_space=pltpu.SMEM)
    far = pl.BlockSpec(memory_space=pltpu.HBM)
    moved = sum(int(np.prod(o.shape)) * o.dtype.itemsize for o in operands)
    return pl.pallas_call(
        kernel,
        out_shape=tuple(jax.ShapeDtypeStruct(shape, dtype) for shape, dtype in outs),
        in_specs=[
            scalar if i in smem else far if i in hbm else vmem for i in range(len(operands))
        ],
        out_specs=tuple(far if i in hbm_outs else vmem for i in range(len(outs))),
        scratch_shapes=list(scratch),
        compiler_params=pltpu.CompilerParams(vmem_limit_bytes=LIMIT * 1024 * 1024),
        cost_estimate=pl.CostEstimate(flops=flops, bytes_accessed=moved, transcendentals=0),
        name=name,
    )(*operands)


def shards(coarse_state, diffusion_number, route_cell, fine_state, fine_diffusion):
    table = jnp.asarray(tables())
    fine_rows = fine_state.reshape(HOSTS, 4, 32, 128).transpose(0, 2, 1, 3).reshape(2048, 128)
    fine_numbers = fine_diffusion.reshape(HOSTS, EDGE**3)

    def exchange(low, high, axis, up_first):
        count = lax.axis_size(axis)
        up = [(i, i + 1) for i in range(count - 1)]
        down = [(i + 1, i) for i in range(count - 1)]
        if up_first:
            from_below = lax.ppermute(high, axis, up)
            return from_below, lax.ppermute(low, axis, down)
        from_above = lax.ppermute(low, axis, down)
        return lax.ppermute(high, axis, up), from_above

    fields = jnp.concatenate([coarse_state, diffusion_number[None]], axis=0)
    first, last = fields[:, :4], fields[:, 4:]
    own = (first, last) + exchange(first, last, "gx", True)
    low, high = call(y_kernel, own, [((320, 128), F32)] * 2, name="y_messages")
    below, above = exchange(low, high, "gy", True)
    everything, low, high = call(
        z_kernel,
        own + (below, above),
        [((1280, 128), F32), ((40, 128), F32), ((40, 128), F32)],
        name="z_messages",
    )
    before, after = exchange(low, high, "gz", False)
    step, early_means, cells = call(
        early_kernel,
        (fine_rows, fine_numbers, table, route_cell.reshape(HOSTS)),
        [((1024, 256), F32), ((HOSTS, 256), F32), ((32, 256), jnp.int32)],
        smem=(3,),
        flops=10**9,
        name="fine_early",
    )
    payload = (HOSTS * SLOT_ROWS, 128)
    sent, full = call(
        half_kernel,
        (everything, before, after, cells, fine_numbers, early_means),
        [(payload, F32), ((4, 8, 8, 128), F32)],
        hbm_outs=(0,),
        scratch=[
            pltpu.VMEM((1280, 256), F32),
            pltpu.VMEM((1024, 256), F32),
            pltpu.VMEM((512, 128), F32),
            pltpu.VMEM(payload, F32),
            pltpu.SemaphoreType.DMA,
        ],
        name="half_step",
    )
    got = lax.all_to_all(
        sent.reshape(HOSTS, SLOT_ROWS, 1, 128), "gz", split_axis=0, concat_axis=0, tiled=True
    ).reshape(payload)
    fine_done, coarse_next = call(
        last_kernel,
        (got, sent, step, fine_rows, fine_numbers, full, cells, table),
        [((2048, 128), F32), ((4, 8, 8, 128), F32)],
        hbm=(1, 2, 3, 4),
        hbm_outs=(0,),
        scratch=[
            pltpu.VMEM(payload, F32),
            pltpu.VMEM((1024, 256), F32),
            pltpu.VMEM((2048, 128), F32),
            pltpu.VMEM((HOSTS, 4096), F32),
            pltpu.VMEM((2048, 128), F32),
            pltpu.SemaphoreType.DMA((5,)),
        ],
        flops=10**9,
        name="last_step",
    )
    fine_next = (
        fine_done.reshape(HOSTS, 32, 4, 128).transpose(0, 2, 1, 3).reshape(fine_state.shape)
    )
    return coarse_next, fine_next


def solution(mesh):
    return jax.shard_map(
        shards,
        mesh=mesh,
        in_specs=(
            P(None, "gx", "gy", "gz"),
            P("gx", "gy", "gz"),
            P("gx", "gy", "gz", None),
            P("gx", "gy", "gz", None, None, None),
            P("gx", "gy", "gz", None, None),
        ),
        out_specs=(P(None, "gx", "gy", "gz"), P("gx", "gy", "gz", None, None, None)),
        check_vma=False,
    )
```

```python
import functools
import math

import jax
import jax.numpy as jnp
import numpy as np
from jax import lax
from jax.experimental import pallas as pl
from jax.experimental.pallas import tpu as pltpu
from jax.sharding import PartitionSpec as P

PB = 4
RATIO = 4
EDGE = PB * RATIO
HOSTS = 16
LIMIT = 16
NUMBER_ROW = 32
MEAN_ROW = 64
FLAG_ROW = 66
SLOT_ROWS = 67
WIND_COARSE = (0.05, 0.03, 0.07)
WIND_PARTS = (5.0, 3.0, 7.0)
ADVECT_UNIT = RATIO * 0.01 / 12.0
F32 = jnp.float32
BF16 = jnp.bfloat16


def interp_table(coarse_count, ratio):
    fine_total = coarse_count * ratio + 4
    weights_table = np.zeros((fine_total, coarse_count + 4), np.float32)
    for fine_index in range(fine_total):
        position = (fine_index - 1.5) / ratio + 2.0
        first_node = math.floor(position - 0.5) - 1
        for offset in range(4):
            weight = 1.0
            for other_node in range(4):
                if other_node != offset:
                    weight = (
                        weight
                        * (position - (first_node + other_node + 0.5))
                        / (offset - other_node)
                    )
            weights_table[fine_index, first_node + offset] = weight
    return weights_table


def high_low(table):
    high = np.asarray(table, np.float32).astype(jnp.bfloat16)
    low = (np.asarray(table, np.float64) - high.astype(np.float64)).astype(jnp.bfloat16)
    return high, low


def tables():
    interp = interp_table(PB, RATIO).astype(np.float64)
    span = EDGE + 4
    lap = np.zeros((span, span, EDGE * EDGE))
    adv = np.zeros((span, span, EDGE * EDGE))
    for y in range(EDGE):
        for z in range(EDGE):
            col = y * EDGE + z
            lap[y + 2, z + 2, col] = -6.0
            for dy, dz, wind in ((1, 0, WIND_PARTS[1]), (0, 1, WIND_PARTS[2])):
                for sign in (1, -1):
                    lap[y + 2 + sign * dy, z + 2 + sign * dz, col] += 1.0
                    adv[y + 2 + sign * dy, z + 2 + sign * dz, col] += sign * 8.0 * wind
                    adv[y + 2 + sign * 2 * dy, z + 2 + sign * 2 * dz, col] -= sign * wind
    inner = np.zeros((span, span), bool)
    inner[2:-2, 2:-2] = True
    inner = inner.reshape(-1)
    both = np.concatenate([lap.reshape(span * span, -1), adv.reshape(span * span, -1)], axis=1)
    spread = np.kron(interp, interp)
    ghost_hi, ghost_lo = high_low(spread.T @ np.where(inner[:, None], 0.0, both))
    face_hi, face_lo = high_low(spread[inner].T)
    mean = np.zeros((EDGE, EDGE, PB, 4, PB, PB), np.float32)
    for y in range(EDGE):
        for z in range(EDGE):
            mean[y, z, z // RATIO, :, :, y // RATIO] = 1.0 / RATIO**3
    copy = np.zeros((4, 2, PB, 2, PB, 2, 4, PB, PB), np.float32)
    for q in range(4):
        for big_x in range(PB):
            for big_y in range(PB):
                copy[q, :, big_x, :, big_y, 0, q, big_x, big_y] = 1.0
    table = np.zeros((5, 256, 512), jnp.bfloat16)
    table[0] = table[1] = both[inner]
    table[2] = np.concatenate([ghost_hi, ghost_lo, ghost_hi, np.zeros_like(ghost_hi)], axis=0)
    table[3, :, :256] = mean.reshape(256, 256)
    table[3, :, 256:] = np.concatenate([face_hi, face_lo, face_hi, np.zeros_like(face_hi)], axis=0)
    table[4, :, :128] = copy.reshape(256, 128)
    return table.reshape(1280, 512)


PLANES = (pl.ds(0, 512), pl.ds(0, 512))
GHOST = (pl.ds(512, 256), pl.ds(0, 512))
PLANES_AND_GHOST = (pl.ds(0, 768), pl.ds(0, 512))
MEAN = (pl.ds(768, 256), pl.ds(0, 256))
FACE = (pl.ds(768, 256), pl.ds(256, 256))
COPY = (pl.ds(1024, 256), pl.ds(0, 128))


def dot(left, right):
    return lax.dot_general(
        left, right, (((1,), (0,)), ((), ())), preferred_element_type=F32
    )


def dot_t(left, right):
    return lax.dot_general(
        left, right, (((1,), (1,)), ((), ())), preferred_element_type=F32
    )


def split(values):
    high = values.astype(BF16)
    return high, (values - high.astype(F32)).astype(BF16)


def is_even(axis):
    return lax.axis_index(axis) % 2 == 0


def x_kernel(coarse_hbm, number_hbm, inner_ref, outer_ref, sems):
    place = jnp.where(is_even("gx"), 4, 0)
    copies = []
    for i, ref in enumerate((outer_ref, inner_ref)):
        at = pl.ds(place if i == 0 else 4 - place, 4)
        copies.append(
            pltpu.make_async_copy(coarse_hbm.at[:, at], ref.at[pl.ds(0, 4)], sems.at[2 * i])
        )
        copies.append(pltpu.make_async_copy(number_hbm.at[at], ref.at[4], sems.at[2 * i + 1]))
    for copy in copies:
        copy.start()
    for copy in copies:
        copy.wait()


def ring_field(inner_ref, outer_ref, far_inner_ref, far_outer_ref, q, x):
    refs = (inner_ref, outer_ref, far_outer_ref, far_inner_ref)
    turned = (outer_ref, inner_ref, far_inner_ref, far_outer_ref)
    even = jnp.broadcast_to(is_even("gx"), (8, 128))
    return jnp.where(even, refs[x // 4][q, x % 4], turned[x // 4][q, x % 4])


def y_kernel(inner_ref, outer_ref, far_inner_ref, far_outer_ref, done_hbm, low_ref, high_ref):
    top = lax.broadcasted_iota(jnp.int32, (8, 128), 0) < 4
    even_y = jnp.broadcast_to(is_even("gy"), (8, 128))
    field = functools.partial(ring_field, inner_ref, outer_ref, far_inner_ref, far_outer_ref)
    for q in range(5):
        for pair in range(8):
            even, odd = field(q, 2 * pair), field(q, 2 * pair + 1)
            at = pl.ds((q * 8 + pair) * 8, 8)
            low = jnp.where(top, even, pltpu.roll(odd, 4, 0))
            high = jnp.where(top, pltpu.roll(even, 4, 0), odd)
            low_ref[at] = jnp.where(even_y, low, high)
            high_ref[at] = jnp.where(even_y, high, low)


def z_kernel(
    inner_ref,
    outer_ref,
    far_inner_ref,
    far_outer_ref,
    far_low_ref,
    far_high_ref,
    done_hbm,
    all_ref,
    low_ref,
    high_ref,
):
    top = lax.broadcasted_iota(jnp.int32, (8, 128), 0) < 4
    even_y = jnp.broadcast_to(is_even("gy"), (8, 128))
    field = functools.partial(ring_field, inner_ref, outer_ref, far_inner_ref, far_outer_ref)
    for q in range(5):
        for pair in range(8):
            at = pl.ds((q * 8 + pair) * 8, 8)
            below = jnp.where(even_y, far_low_ref[at], far_high_ref[at])
            above = jnp.where(even_y, far_high_ref[at], far_low_ref[at])
            row = (q * 16 + 2 * pair) * 16
            all_ref[pl.ds(row, 8)] = field(q, 2 * pair)
            all_ref[pl.ds(row + 8, 8)] = jnp.where(top, above, pltpu.roll(below, 4, 0))
            all_ref[pl.ds(row + 16, 8)] = field(q, 2 * pair + 1)
            all_ref[pl.ds(row + 24, 8)] = jnp.where(top, pltpu.roll(above, 4, 0), below)
    group = lax.broadcasted_iota(jnp.int32, (40, 128), 1) // 4
    low = jnp.zeros((40, 128), F32)
    high = jnp.zeros((40, 128), F32)
    for g in range(32):
        rows = all_ref[pl.ds(g * 40, 40)]
        low = jnp.where(group == g, pltpu.roll(rows, 4 * g, 1) if g else rows, low)
        shift = (4 * g + 4) % 128
        high = jnp.where(group == g, pltpu.roll(rows, shift, 1) if shift else rows, high)
    even_z = jnp.broadcast_to(is_even("gz"), (40, 128))
    low_ref[...] = jnp.where(even_z, low, high)
    high_ref[...] = jnp.where(even_z, high, low)


def rate_parts(center, x_near, x_far, y_axis, wind):
    rows, lanes = center.shape
    y_up, y_down = pltpu.roll(center, rows - 1, y_axis), pltpu.roll(center, 1, y_axis)
    y_up2, y_down2 = pltpu.roll(center, rows - 2, y_axis), pltpu.roll(center, 2, y_axis)
    z_up, z_down = pltpu.roll(center, lanes - 1, 1), pltpu.roll(center, 1, 1)
    z_up2, z_down2 = pltpu.roll(center, lanes - 2, 1), pltpu.roll(center, 2, 1)
    laplace = (
        (x_near[0] + x_near[1]) + (y_up + y_down) + (z_up + z_down) - 6.0 * center
    )
    advect = (
        (wind[0] / 12.0) * (8.0 * (x_near[0] - x_near[1]) - (x_far[0] - x_far[1]))
        + (wind[1] / 12.0) * (8.0 * (y_up - y_down) - (y_up2 - y_down2))
        + (wind[2] / 12.0) * (8.0 * (z_up - z_down) - (z_up2 - z_down2))
    )
    return laplace, advect


HALF_PLACES = tuple(range(10)) + (14, 15)
WINDOW_PLACES = (14, 15) + tuple(range(10))


def half_kernel(
    all_ref,
    far_low_ref,
    far_high_ref,
    cells_ref,
    number_ref,
    mean_ref,
    more_ref,
    sent_ref,
    full_ref,
    now_ref,
    half_ref,
    cut_ref,
    pay_ref,
    sem,
):
    lane40 = lax.broadcasted_iota(jnp.int32, (40, 128), 1)
    even_z = jnp.broadcast_to(is_even("gz"), (40, 128))
    before = jnp.where(even_z, far_low_ref[...], far_high_ref[...])
    after = jnp.where(even_z, far_high_ref[...], far_low_ref[...])
    for g in range(32):
        ahead = pltpu.roll(after, (128 - 4 * g) % 128, 1) if g else after
        shift = (124 - 4 * g) % 128
        behind = pltpu.roll(before, shift, 1) if shift else before
        rows = pl.ds(g * 40, 40)
        now_ref[rows, pl.ds(0, 128)] = all_ref[rows]
        now_ref[rows, pl.ds(128, 128)] = jnp.where(
            lane40 < 4, ahead, jnp.where(lane40 >= 124, behind, 0.0)
        )

    def sheet(q, x):
        return now_ref[pl.ds((q * 16 + x) * 16, 16)]

    for x in HALF_PLACES:
        number = sheet(4, x)
        for q in range(4):
            center = sheet(q, x)
            near = (sheet(q, (x + 1) % 16), sheet(q, (x - 1) % 16))
            far = (sheet(q, (x + 2) % 16), sheet(q, (x - 2) % 16))
            laplace, advect = rate_parts(center, near, far, 0, WIND_COARSE)
            stepped = center + number * laplace - advect
            half_ref[pl.ds((q * 16 + x) * 16, 16)] = jnp.where(number > 0.0, stepped, 0.0)

    cells = cells_ref[pl.ds(0, 1), pl.ds(0, 128)]
    lane = lax.broadcasted_iota(jnp.int32, (1, 128), 1)
    wanted = (4 * (cells & 31) - 2 + (lane & 7)) & 255
    place = lax.broadcasted_iota(jnp.int32, (256, 128), 0)
    pick = jnp.where((place == wanted) & (cells >= 0), 1.0, 0.0).astype(BF16)
    far_x = jnp.broadcast_to(((cells >> 6) & 1) == 1, (16, 128))
    far_y = jnp.broadcast_to(((cells >> 5) & 1) == 1, (8, 128))
    for t, field_ref in enumerate((now_ref, half_ref)):
        for q in range(4):
            cut = []
            for first, count in ((14, 2), (0, 10)):
                high, low = split(field_ref[pl.ds((q * 16 + first) * 16, count * 16)])
                cut.append(dot(high, pick) + dot(low, pick))
            cut = jnp.concatenate(cut, axis=0)
            for i in range(8):
                rows = jnp.where(
                    far_x, cut[(i + 4) * 16 : (i + 5) * 16], cut[i * 16 : (i + 1) * 16]
                )
                near_rows = pltpu.roll(rows, 2, 0)[:8]
                far_rows = pltpu.roll(rows, 14, 0)[:8]
                cut_ref[pl.ds(((t * 4 + q) * 8 + i) * 8, 8)] = jnp.where(
                    far_y, far_rows, near_rows
                )
    group = lax.broadcasted_iota(jnp.int32, (32, 128), 1) // 8
    pieces = [
        cut_ref[pl.ds(t * 256 + y, 32, stride=8)] for t in range(2) for y in range(8)
    ]
    for step in (8, 4, 2, 1):
        swap = (group & step) != 0
        for i in range(16):
            if not i & step:
                a, b = pieces[i], pieces[i + step]
                pieces[i] = jnp.where(swap, pltpu.roll(b, 8 * step, 1), a)
                pieces[i + step] = jnp.where(swap, b, pltpu.roll(a, 128 - 8 * step, 1))
    for slot in range(HOSTS):
        pay_ref[pl.ds(slot * SLOT_ROWS, 32)] = pieces[slot]
    for column in range(32):
        pay_ref[pl.ds(NUMBER_ROW + column, HOSTS, stride=SLOT_ROWS)] = number_ref[
            :, pl.ds(column * 128, 128)
        ]
    for side in range(2):
        pay_ref[pl.ds(MEAN_ROW + side, HOSTS, stride=SLOT_ROWS)] = (
            mean_ref[:, pl.ds(side * 128, 128)] + more_ref[:, pl.ds(side * 128, 128)]
        )
    placed = cells_ref[pl.ds(16, HOSTS), pl.ds(0, 128)] >= 0
    pay_ref[pl.ds(FLAG_ROW, HOSTS, stride=SLOT_ROWS)] = jnp.where(placed, 1.0, 0.0)
    copy = pltpu.make_async_copy(pay_ref, sent_ref, sem)
    copy.start()
    full_step(now_ref, half_ref, cells_ref, full_ref)
    copy.wait()


def full_step(now_ref, half_ref, cells_ref, full_ref):
    lane = lax.broadcasted_iota(jnp.int32, (HOSTS, 128), 1)
    top = lax.broadcasted_iota(jnp.int32, (8, 128), 0) < 4
    cells = cells_ref[pl.ds(16, HOSTS), pl.ds(0, 128)]
    hit = (lane >> 2) == (cells & 31)
    covered = [
        jnp.max(jnp.where(hit & ((cells >> 5) == corner), 1, 0), axis=0, keepdims=True)
        for corner in range(4)
    ]

    def sheet(q, x):
        return half_ref[pl.ds((q * 16 + x % 16) * 16, 16)]

    for x in range(8):
        keep = jnp.where(top, covered[(x // 4) * 2], covered[(x // 4) * 2 + 1]) == 0
        number = now_ref[pl.ds((64 + x) * 16, 8), pl.ds(0, 128)]
        for q in range(4):
            center = sheet(q, x)
            laplace, advect = rate_parts(
                center,
                (sheet(q, x + 1), sheet(q, x - 1)),
                (sheet(q, x + 2), sheet(q, x - 2)),
                0,
                WIND_COARSE,
            )
            done = 0.5 * (
                now_ref[pl.ds((q * 16 + x) * 16, 8), pl.ds(0, 128)]
                + center[:8, :128]
                + number * laplace[:8, :128]
                - advect[:8, :128]
            )
            full_ref[q, x] = jnp.where(keep, done, 0.0)


def put_means(back, full_ref, cells_ref, table_ref, next_ref):
    even, odd = back[:, :128], back[:, 128:]
    values = jnp.concatenate(
        [even, pltpu.roll(even, 64, 1), odd, pltpu.roll(odd, 64, 1)], axis=0
    )
    high = values.astype(BF16)
    low, lowest = split(values - high.astype(F32))
    parts = jnp.concatenate([high, low, lowest, jnp.zeros_like(high)], axis=0)
    spread = dot_t(table_ref[COPY], parts)
    cells = cells_ref[pl.ds(8, 1)]
    row = lax.broadcasted_iota(jnp.int32, (256, 1), 0)
    corner = ((row >> 5) & 1) * 2 + ((row >> 2) & 1)
    spread = jnp.where((cells >> 5) == corner, spread, 0.0).astype(BF16)
    z = lax.broadcasted_iota(jnp.int32, (128, 256), 0)
    lane = lax.broadcasted_iota(jnp.int32, (128, 256), 1)
    here = ((z >> 2) == (cells & 31)) & ((z & 3) == ((lane >> 4) & 3)) & (cells >= 0)
    added = dot_t(spread, jnp.where(here, 1.0, 0.0).astype(BF16))
    for q in range(4):
        for x in range(8):
            at = (q * 8 + x) * 8
            next_ref[q, x] = full_ref[q, x] + added[at : at + 8]


def plane_parts(field, table_ref):
    both = dot(jnp.concatenate(split(field), axis=1), table_ref[PLANES])
    return both[:, :256], both[:, 256:]


def plus(left, right):
    if left is None or right is None:
        return right if left is None else left
    return left + right


def minus(left, right):
    if right is None:
        return left
    return -right if left is None else left - right


def x_parts(padded):
    laplace, advect = [], []
    for x in range(2, 18):
        near = minus(padded[x + 1], padded[x - 1])
        far = minus(padded[x + 2], padded[x - 2])
        laplace.append(plus(padded[x + 1], padded[x - 1]))
        near = None if near is None else (8.0 * WIND_PARTS[0]) * near
        far = None if far is None else WIND_PARTS[0] * far
        advect.append(minus(near, far))
    return laplace, advect


def plane(values, x):
    return values[x * HOSTS : (x + 1) * HOSTS]


def rate_of(numbers, padded, laplace, advect):
    x_laplace, x_advect = x_parts(padded)
    return [
        numbers[x] * plus(x_laplace[x], plane(laplace, x))
        - ADVECT_UNIT * plus(x_advect[x], plane(advect, x))
        for x in range(EDGE)
    ]


def means(planes, table_ref):
    sums = []
    for big_x in range(PB):
        group = planes[big_x * 4 : big_x * 4 + 4]
        sums.append((group[0] + group[1]) + (group[2] + group[3]))
    high, low = split(jnp.concatenate(sums, axis=0))
    every = dot(high, table_ref[MEAN]) + dot(low, table_ref[MEAN])
    lane_x = (lax.broadcasted_iota(jnp.int32, (HOSTS, 256), 1) >> 2) & 3
    total = plane(every, 0)
    for big_x in range(1, PB):
        total = jnp.where(lane_x == big_x, plane(every, big_x), total)
    return total


def lane_of_q():
    return (lax.broadcasted_iota(jnp.int32, (HOSTS, 256), 1) >> 4) & 3


def early_kernel(fields, fine_ref, number_ref, table_ref, after_hbm, step_ref, back_ref):
    numbers = [number_ref[:, pl.ds(x * 256, 256)] for x in range(EDGE)]
    nothing = [None, None]
    back = jnp.zeros((HOSTS, 256), F32)
    for q in fields:
        planes = []
        for x in range(EDGE):
            sides = [
                fine_ref[pl.ds((2 * x + side) * 4 + q, HOSTS, stride=128)] for side in range(2)
            ]
            planes.append(jnp.concatenate(sides, axis=1))
        parts = plane_parts(jnp.concatenate(planes, axis=0), table_ref)
        rate = rate_of(numbers, nothing + planes + nothing, *parts)
        half = [planes[x] + rate[x] for x in range(EDGE)]
        parts = plane_parts(jnp.concatenate(half, axis=0), table_ref)
        rate = rate_of(numbers, nothing + half + nothing, *parts)
        done = [0.5 * (planes[x] + half[x] + rate[x]) for x in range(EDGE)]
        for x in range(EDGE):
            step_ref[pl.ds(((q - fields[0]) * EDGE + x) * HOSTS, HOSTS)] = done[x]
        back = jnp.where(lane_of_q() == q, means(done, table_ref), back)
    back_ref[...] = back


def cells_kernel(route_ref, after_hbm, cells_ref):
    lane = lax.broadcasted_iota(jnp.int32, (8, 256), 1)
    row = lax.broadcasted_iota(jnp.int32, (HOSTS, 256), 0)
    by_eight = jnp.zeros((8, 256), jnp.int32)
    by_one = jnp.zeros((8, 256), jnp.int32)
    by_row = jnp.zeros((HOSTS, 256), jnp.int32)
    for slot in range(HOSTS):
        cell = route_ref[slot]
        by_eight = jnp.where(((lane >> 3) & 15) == slot, cell, by_eight)
        by_one = jnp.where((lane & 15) == slot, cell, by_one)
        by_row = jnp.where(row == slot, cell, by_row)
    cells_ref[pl.ds(0, 8)] = by_eight
    cells_ref[pl.ds(8, 8)] = by_one
    cells_ref[pl.ds(16, HOSTS)] = by_row


def ghosts(block_ref, q, t, table_ref):
    interp = interp_table(PB, RATIO)
    first_half = lax.broadcasted_iota(jnp.int32, (HOSTS, 128), 1) < 64
    coarse = []
    for x in range(8):
        rows = block_ref[pl.ds(q * 8 + x, HOSTS, stride=SLOT_ROWS)]
        turned = pltpu.roll(rows, 64, 1)
        coarse.append(
            jnp.where(first_half, rows, turned) if t == 0 else jnp.where(first_half, turned, rows)
        )
    inner, outer = [], []
    for i in range(EDGE + 4):
        total = None
        for j in range(8):
            if interp[i, j] != 0.0:
                total = plus(total, float(interp[i, j]) * coarse[j])
        (inner if 2 <= i < EDGE + 2 else outer).append(total)
    inner = jnp.concatenate(split(jnp.concatenate(inner, axis=0)), axis=1)
    faces = dot(jnp.concatenate(split(jnp.concatenate(outer, axis=0)), axis=1), table_ref[FACE])
    return inner, [plane(faces, i) for i in range(4)]


def ghost_part(block_ref, numbers, q, table_ref):
    inner, faces = ghosts(block_ref, q, 0, table_ref)
    both = dot(inner, table_ref[GHOST])
    half = rate_of(
        numbers, faces[:2] + [None] * EDGE + faces[2:], both[:, :256], both[:, 256:]
    )
    inner, faces = ghosts(block_ref, q, 1, table_ref)
    fields = split(jnp.concatenate(half, axis=0)) + (inner,)
    both = dot(jnp.concatenate(fields, axis=1), table_ref[PLANES_AND_GHOST])
    rate = rate_of(numbers, faces[:2] + half + faces[2:], both[:, :256], both[:, 256:])
    return [0.5 * (half[x] + rate[x]) for x in range(EDGE)]


def last_kernel(
    got_ref,
    sent_hbm,
    step_hbm,
    more_hbm,
    old_hbm,
    number_hbm,
    full_ref,
    cells_ref,
    table_ref,
    fine_hbm,
    next_ref,
    sent_ref,
    step_ref,
    old_ref,
    number_ref,
    fine_ref,
    sems,
):
    copies = [
        pltpu.make_async_copy(src, dst, sems.at[i])
        for i, (src, dst) in enumerate(
            (
                (number_hbm, number_ref),
                (step_hbm, step_ref.at[pl.ds(0, 512)]),
                (more_hbm, step_ref.at[pl.ds(512, 512)]),
                (old_hbm, old_ref),
                (sent_hbm, sent_ref),
            )
        )
    ]
    for copy in copies:
        copy.start()

    def got(row):
        sides = [got_ref[pl.ds(row + side, HOSTS, stride=SLOT_ROWS)] for side in range(2)]
        return jnp.concatenate(sides, axis=1)

    placed = got_ref[pl.ds(FLAG_ROW, HOSTS, stride=SLOT_ROWS)] > 0.5
    copies[0].wait()
    numbers = [number_ref[:, pl.ds(x * 256, 256)] for x in range(EDGE)]
    for q in range(4):
        added = ghost_part(got_ref, numbers, q, table_ref)
        if q == 0:
            for copy in copies[1:4]:
                copy.wait()
        for x in range(EDGE):
            done = step_ref[pl.ds((q * EDGE + x) * HOSTS, HOSTS)] + added[x]
            for side in range(2):
                at = pl.ds((2 * x + side) * 4 + q, HOSTS, stride=128)
                fine_ref[at] = jnp.where(
                    placed, done[:, side * 128 : side * 128 + 128], old_ref[at]
                )
    out = pltpu.make_async_copy(fine_ref, fine_hbm, sems.at[5])
    out.start()
    copies[4].wait()
    numbers = [got(NUMBER_ROW + 2 * x) for x in range(EDGE)]
    back = jnp.zeros((HOSTS, 256), F32)
    for q in range(4):
        added = ghost_part(sent_ref, numbers, q, table_ref)
        back = jnp.where(lane_of_q() == q, means(added, table_ref), back)
    put_means(back + got(MEAN_ROW), full_ref, cells_ref, table_ref, next_ref)
    out.wait()


def call(kernel, operands, outs, smem=(), hbm=(), hbm_outs=(), scratch=(), flops=10**6, name=None):
    vmem = pl.BlockSpec(memory_space=pltpu.VMEM)
    scalar = pl.BlockSpec(memory_space=pltpu.SMEM)
    far = pl.BlockSpec(memory_space=pltpu.HBM)
    moved = sum(int(np.prod(o.shape)) * o.dtype.itemsize for o in operands)
    return pl.pallas_call(
        kernel,
        out_shape=tuple(jax.ShapeDtypeStruct(shape, dtype) for shape, dtype in outs),
        in_specs=[
            scalar if i in smem else far if i in hbm else vmem for i in range(len(operands))
        ],
        out_specs=tuple(far if i in hbm_outs else vmem for i in range(len(outs))),
        scratch_shapes=list(scratch),
        compiler_params=pltpu.CompilerParams(vmem_limit_bytes=LIMIT * 1024 * 1024),
        cost_estimate=pl.CostEstimate(flops=flops, bytes_accessed=moved, transcendentals=0),
        name=name,
    )(*operands)


def shards(coarse_state, diffusion_number, route_cell, fine_state, fine_diffusion):
    table = jnp.asarray(tables())
    fine_rows = fine_state.reshape(HOSTS, 4, 32, 128).transpose(0, 2, 1, 3).reshape(2048, 128)
    fine_numbers = fine_diffusion.reshape(HOSTS, EDGE**3)

    def swap(inner, outer, axis):
        count = lax.axis_size(axis)
        pairs = [[], []]
        for i in range(count - 1):
            pairs[i % 2] += [(i, i + 1), (i + 1, i)]
        return lax.ppermute(inner, axis, pairs[1]), lax.ppermute(outer, axis, pairs[0])

    inner, outer = call(
        x_kernel,
        (coarse_state, diffusion_number),
        [((5, 4, 8, 128), F32)] * 2,
        hbm=(0, 1),
        scratch=[pltpu.SemaphoreType.DMA((4,))],
        name="x_messages",
    )
    own = (inner, outer) + swap(inner, outer, "gx")

    def early(fields, after):
        return call(
            functools.partial(early_kernel, fields),
            (fine_rows, fine_numbers, table, after),
            [((len(fields) * 256, 256), F32), ((HOSTS, 256), F32)],
            hbm=(3,),
            flops=10**9,
            name="fine_early",
        )

    step, back = early((0, 1), own[2])
    low, high = call(y_kernel, own + (back,), [((320, 128), F32)] * 2, hbm=(4,), name="y_messages")
    more_step, more_back = early((2, 3), low)
    everything, low, high = call(
        z_kernel,
        own + swap(low, high, "gy") + (more_back,),
        [((1280, 128), F32), ((40, 128), F32), ((40, 128), F32)],
        hbm=(6,),
        name="z_messages",
    )
    far_low, far_high = swap(low, high, "gz")
    (cells,) = call(
        cells_kernel,
        (route_cell.reshape(HOSTS), everything),
        [((32, 256), jnp.int32)],
        smem=(0,),
        hbm=(1,),
        name="cells",
    )
    payload = (HOSTS * SLOT_ROWS, 128)
    sent, full = call(
        half_kernel,
        (everything, far_low, far_high, cells, fine_numbers, back, more_back),
        [(payload, F32), ((4, 8, 8, 128), F32)],
        hbm_outs=(0,),
        scratch=[
            pltpu.VMEM((1280, 256), F32),
            pltpu.VMEM((1024, 256), F32),
            pltpu.VMEM((512, 128), F32),
            pltpu.VMEM(payload, F32),
            pltpu.SemaphoreType.DMA,
        ],
        name="half_step",
    )
    got = lax.all_to_all(
        sent.reshape(HOSTS, SLOT_ROWS, 1, 128), "gz", split_axis=0, concat_axis=0, tiled=True
    ).reshape(payload)
    fine_done, coarse_next = call(
        last_kernel,
        (got, sent, step, more_step, fine_rows, fine_numbers, full, cells, table),
        [((2048, 128), F32), ((4, 8, 8, 128), F32)],
        hbm=(1, 2, 3, 4, 5),
        hbm_outs=(0,),
        scratch=[
            pltpu.VMEM(payload, F32),
            pltpu.VMEM((1024, 256), F32),
            pltpu.VMEM((2048, 128), F32),
            pltpu.VMEM((HOSTS, 4096), F32),
            pltpu.VMEM((2048, 128), F32),
            pltpu.SemaphoreType.DMA((6,)),
        ],
        flops=10**9,
        name="last_step",
    )
    fine_next = (
        fine_done.reshape(HOSTS, 32, 4, 128).transpose(0, 2, 1, 3).reshape(fine_state.shape)
    )
    return coarse_next, fine_next


def solution(mesh):
    return jax.shard_map(
        shards,
        mesh=mesh,
        in_specs=(
            P(None, "gx", "gy", "gz"),
            P("gx", "gy", "gz"),
            P("gx", "gy", "gz", None),
            P("gx", "gy", "gz", None, None, None),
            P("gx", "gy", "gz", None, None),
        ),
        out_specs=(P(None, "gx", "gy", "gz"), P("gx", "gy", "gz", None, None, None)),
        check_vma=False,
    )
```

```python
import functools
import math

import jax
import jax.numpy as jnp
import numpy as np
from jax import lax
from jax.experimental import pallas as pl
from jax.experimental.pallas import tpu as pltpu
from jax.sharding import PartitionSpec as P

PB = 4
RATIO = 4
EDGE = PB * RATIO
HOSTS = 16
TOGETHER = 4
LIMIT = 16
NUMBER_ROW = 32
MEAN_ROW = 64
FLAG_ROW = 66
SLOT_ROWS = 67
WIND_COARSE = (0.05, 0.03, 0.07)
WIND_PARTS = (5.0, 3.0, 7.0)
ADVECT_UNIT = RATIO * 0.01 / 12.0
F32 = jnp.float32
BF16 = jnp.bfloat16


def interp_table(coarse_count, ratio):
    fine_total = coarse_count * ratio + 4
    weights_table = np.zeros((fine_total, coarse_count + 4), np.float32)
    for fine_index in range(fine_total):
        position = (fine_index - 1.5) / ratio + 2.0
        first_node = math.floor(position - 0.5) - 1
        for offset in range(4):
            weight = 1.0
            for other_node in range(4):
                if other_node != offset:
                    weight = (
                        weight
                        * (position - (first_node + other_node + 0.5))
                        / (offset - other_node)
                    )
            weights_table[fine_index, first_node + offset] = weight
    return weights_table


def high_low(table):
    high = np.asarray(table, np.float32).astype(jnp.bfloat16)
    low = (np.asarray(table, np.float64) - high.astype(np.float64)).astype(jnp.bfloat16)
    return high, low


def tables():
    interp = interp_table(PB, RATIO).astype(np.float64)
    span = EDGE + 4
    lap = np.zeros((span, span, EDGE * EDGE))
    adv = np.zeros((span, span, EDGE * EDGE))
    for y in range(EDGE):
        for z in range(EDGE):
            col = y * EDGE + z
            lap[y + 2, z + 2, col] = -6.0
            for dy, dz, wind in ((1, 0, WIND_PARTS[1]), (0, 1, WIND_PARTS[2])):
                for sign in (1, -1):
                    lap[y + 2 + sign * dy, z + 2 + sign * dz, col] += 1.0
                    adv[y + 2 + sign * dy, z + 2 + sign * dz, col] += sign * 8.0 * wind
                    adv[y + 2 + sign * 2 * dy, z + 2 + sign * 2 * dz, col] -= sign * wind
    inner = np.zeros((span, span), bool)
    inner[2:-2, 2:-2] = True
    inner = inner.reshape(-1)
    both = np.concatenate([lap.reshape(span * span, -1), adv.reshape(span * span, -1)], axis=1)
    spread = np.kron(interp, interp)
    ghost_hi, ghost_lo = high_low(spread.T @ np.where(inner[:, None], 0.0, both))
    face_hi, face_lo = high_low(spread[inner].T)
    mean = np.zeros((EDGE, EDGE, PB, 4, PB, PB), np.float32)
    for y in range(EDGE):
        for z in range(EDGE):
            mean[y, z, z // RATIO, :, :, y // RATIO] = 1.0 / RATIO**3
    copy = np.zeros((4, 2, PB, 2, PB, 2, 4, PB, PB), np.float32)
    for q in range(4):
        for big_x in range(PB):
            for big_y in range(PB):
                copy[q, :, big_x, :, big_y, 0, q, big_x, big_y] = 1.0
    table = np.zeros((5, 256, 512), jnp.bfloat16)
    table[0] = table[1] = both[inner]
    table[2] = np.concatenate([ghost_hi, ghost_lo, ghost_hi, np.zeros_like(ghost_hi)], axis=0)
    table[3, :, :256] = mean.reshape(256, 256)
    table[3, :, 256:] = np.concatenate([face_hi, face_lo, face_hi, np.zeros_like(face_hi)], axis=0)
    table[4, :, :128] = copy.reshape(256, 128)
    return table.reshape(1280, 512)


PLANES = (pl.ds(0, 512), pl.ds(0, 512))
GHOST = (pl.ds(512, 256), pl.ds(0, 512))
PLANES_AND_GHOST = (pl.ds(0, 768), pl.ds(0, 512))
MEAN = (pl.ds(768, 256), pl.ds(0, 256))
FACE = (pl.ds(768, 256), pl.ds(256, 256))
COPY = (pl.ds(1024, 256), pl.ds(0, 128))


def dot(left, right):
    return lax.dot_general(
        left, right, (((1,), (0,)), ((), ())), preferred_element_type=F32
    )


def dot_t(left, right):
    return lax.dot_general(
        left, right, (((1,), (1,)), ((), ())), preferred_element_type=F32
    )


def split(values):
    high = values.astype(BF16)
    return high, (values - high.astype(F32)).astype(BF16)


def is_even(axis):
    return lax.axis_index(axis) % 2 == 0


def x_kernel(first_ref, last_ref, inner_ref, outer_ref):
    even = jnp.broadcast_to(is_even("gx"), (8, 128))
    for q in range(5):
        for x in range(4):
            first, last = first_ref[q, x], last_ref[q, x]
            inner_ref[q, x] = jnp.where(even, first, last)
            outer_ref[q, x] = jnp.where(even, last, first)


def ring_field(inner_ref, outer_ref, far_inner_ref, far_outer_ref, q, x):
    refs = (inner_ref, outer_ref, far_outer_ref, far_inner_ref)
    turned = (outer_ref, inner_ref, far_inner_ref, far_outer_ref)
    even = jnp.broadcast_to(is_even("gx"), (8, 128))
    return jnp.where(even, refs[x // 4][q, x % 4], turned[x // 4][q, x % 4])


def y_kernel(inner_ref, outer_ref, far_inner_ref, far_outer_ref, done_hbm, low_ref, high_ref):
    top = lax.broadcasted_iota(jnp.int32, (8, 128), 0) < 4
    even_y = jnp.broadcast_to(is_even("gy"), (8, 128))
    field = functools.partial(ring_field, inner_ref, outer_ref, far_inner_ref, far_outer_ref)
    for q in range(5):
        for pair in range(8):
            even, odd = field(q, 2 * pair), field(q, 2 * pair + 1)
            at = pl.ds((q * 8 + pair) * 8, 8)
            low = jnp.where(top, even, pltpu.roll(odd, 4, 0))
            high = jnp.where(top, pltpu.roll(even, 4, 0), odd)
            low_ref[at] = jnp.where(even_y, low, high)
            high_ref[at] = jnp.where(even_y, high, low)


def z_kernel(
    inner_ref,
    outer_ref,
    far_inner_ref,
    far_outer_ref,
    far_low_ref,
    far_high_ref,
    done_hbm,
    all_ref,
    low_ref,
    high_ref,
):
    top = lax.broadcasted_iota(jnp.int32, (8, 128), 0) < 4
    even_y = jnp.broadcast_to(is_even("gy"), (8, 128))
    field = functools.partial(ring_field, inner_ref, outer_ref, far_inner_ref, far_outer_ref)
    for q in range(5):
        for pair in range(8):
            at = pl.ds((q * 8 + pair) * 8, 8)
            below = jnp.where(even_y, far_low_ref[at], far_high_ref[at])
            above = jnp.where(even_y, far_high_ref[at], far_low_ref[at])
            row = (q * 16 + 2 * pair) * 16
            all_ref[pl.ds(row, 8)] = field(q, 2 * pair)
            all_ref[pl.ds(row + 8, 8)] = jnp.where(top, above, pltpu.roll(below, 4, 0))
            all_ref[pl.ds(row + 16, 8)] = field(q, 2 * pair + 1)
            all_ref[pl.ds(row + 24, 8)] = jnp.where(top, pltpu.roll(above, 4, 0), below)
    group = lax.broadcasted_iota(jnp.int32, (40, 128), 1) // 4
    low = jnp.zeros((40, 128), F32)
    high = jnp.zeros((40, 128), F32)
    for g in range(32):
        rows = all_ref[pl.ds(g * 40, 40)]
        low = jnp.where(group == g, pltpu.roll(rows, 4 * g, 1) if g else rows, low)
        shift = (4 * g + 4) % 128
        high = jnp.where(group == g, pltpu.roll(rows, shift, 1) if shift else rows, high)
    even_z = jnp.broadcast_to(is_even("gz"), (40, 128))
    low_ref[...] = jnp.where(even_z, low, high)
    high_ref[...] = jnp.where(even_z, high, low)


def rate_parts(center, x_near, x_far, y_axis, wind):
    rows, lanes = center.shape
    y_up, y_down = pltpu.roll(center, rows - 1, y_axis), pltpu.roll(center, 1, y_axis)
    y_up2, y_down2 = pltpu.roll(center, rows - 2, y_axis), pltpu.roll(center, 2, y_axis)
    z_up, z_down = pltpu.roll(center, lanes - 1, 1), pltpu.roll(center, 1, 1)
    z_up2, z_down2 = pltpu.roll(center, lanes - 2, 1), pltpu.roll(center, 2, 1)
    laplace = (
        (x_near[0] + x_near[1]) + (y_up + y_down) + (z_up + z_down) - 6.0 * center
    )
    advect = (
        (wind[0] / 12.0) * (8.0 * (x_near[0] - x_near[1]) - (x_far[0] - x_far[1]))
        + (wind[1] / 12.0) * (8.0 * (y_up - y_down) - (y_up2 - y_down2))
        + (wind[2] / 12.0) * (8.0 * (z_up - z_down) - (z_up2 - z_down2))
    )
    return laplace, advect


HALF_PLACES = tuple(range(10)) + (14, 15)
WINDOW_PLACES = (14, 15) + tuple(range(10))


def half_kernel(
    all_ref,
    far_low_ref,
    far_high_ref,
    cells_ref,
    number_ref,
    mean_ref,
    sent_ref,
    full_ref,
    now_ref,
    half_ref,
    cut_ref,
    pay_ref,
    sem,
):
    lane40 = lax.broadcasted_iota(jnp.int32, (40, 128), 1)
    even_z = jnp.broadcast_to(is_even("gz"), (40, 128))
    before = jnp.where(even_z, far_low_ref[...], far_high_ref[...])
    after = jnp.where(even_z, far_high_ref[...], far_low_ref[...])
    for g in range(32):
        ahead = pltpu.roll(after, (128 - 4 * g) % 128, 1) if g else after
        shift = (124 - 4 * g) % 128
        behind = pltpu.roll(before, shift, 1) if shift else before
        rows = pl.ds(g * 40, 40)
        now_ref[rows, pl.ds(0, 128)] = all_ref[rows]
        now_ref[rows, pl.ds(128, 128)] = jnp.where(
            lane40 < 4, ahead, jnp.where(lane40 >= 124, behind, 0.0)
        )

    def sheet(q, x):
        return now_ref[pl.ds((q * 16 + x) * 16, 16)]

    for x in HALF_PLACES:
        number = sheet(4, x)
        for q in range(4):
            center = sheet(q, x)
            near = (sheet(q, (x + 1) % 16), sheet(q, (x - 1) % 16))
            far = (sheet(q, (x + 2) % 16), sheet(q, (x - 2) % 16))
            laplace, advect = rate_parts(center, near, far, 0, WIND_COARSE)
            stepped = center + number * laplace - advect
            half_ref[pl.ds((q * 16 + x) * 16, 16)] = jnp.where(number > 0.0, stepped, 0.0)

    cells = cells_ref[pl.ds(0, 1), pl.ds(0, 128)]
    lane = lax.broadcasted_iota(jnp.int32, (1, 128), 1)
    wanted = (4 * (cells & 31) - 2 + (lane & 7)) & 255
    place = lax.broadcasted_iota(jnp.int32, (256, 128), 0)
    pick = jnp.where((place == wanted) & (cells >= 0), 1.0, 0.0).astype(BF16)
    far_x = jnp.broadcast_to(((cells >> 6) & 1) == 1, (16, 128))
    far_y = jnp.broadcast_to(((cells >> 5) & 1) == 1, (8, 128))
    for t, field_ref in enumerate((now_ref, half_ref)):
        for q in range(4):
            cut = []
            for first, count in ((14, 2), (0, 10)):
                high, low = split(field_ref[pl.ds((q * 16 + first) * 16, count * 16)])
                cut.append(dot(high, pick) + dot(low, pick))
            cut = jnp.concatenate(cut, axis=0)
            for i in range(8):
                rows = jnp.where(
                    far_x, cut[(i + 4) * 16 : (i + 5) * 16], cut[i * 16 : (i + 1) * 16]
                )
                near_rows = pltpu.roll(rows, 2, 0)[:8]
                far_rows = pltpu.roll(rows, 14, 0)[:8]
                cut_ref[pl.ds(((t * 4 + q) * 8 + i) * 8, 8)] = jnp.where(
                    far_y, far_rows, near_rows
                )
    group = lax.broadcasted_iota(jnp.int32, (32, 128), 1) // 8
    pieces = [
        cut_ref[pl.ds(t * 256 + y, 32, stride=8)] for t in range(2) for y in range(8)
    ]
    for step in (8, 4, 2, 1):
        swap = (group & step) != 0
        for i in range(16):
            if not i & step:
                a, b = pieces[i], pieces[i + step]
                pieces[i] = jnp.where(swap, pltpu.roll(b, 8 * step, 1), a)
                pieces[i + step] = jnp.where(swap, b, pltpu.roll(a, 128 - 8 * step, 1))
    for slot in range(HOSTS):
        pay_ref[pl.ds(slot * SLOT_ROWS, 32)] = pieces[slot]
    for column in range(32):
        pay_ref[pl.ds(NUMBER_ROW + column, HOSTS, stride=SLOT_ROWS)] = number_ref[
            :, pl.ds(column * 128, 128)
        ]
    for side in range(2):
        pay_ref[pl.ds(MEAN_ROW + side, HOSTS, stride=SLOT_ROWS)] = mean_ref[
            :, pl.ds(side * 128, 128)
        ]
    placed = cells_ref[pl.ds(16, HOSTS), pl.ds(0, 128)] >= 0
    pay_ref[pl.ds(FLAG_ROW, HOSTS, stride=SLOT_ROWS)] = jnp.where(placed, 1.0, 0.0)
    copy = pltpu.make_async_copy(pay_ref, sent_ref, sem)
    copy.start()
    full_step(now_ref, half_ref, cells_ref, full_ref)
    copy.wait()


def full_step(now_ref, half_ref, cells_ref, full_ref):
    lane = lax.broadcasted_iota(jnp.int32, (HOSTS, 128), 1)
    top = lax.broadcasted_iota(jnp.int32, (8, 128), 0) < 4
    cells = cells_ref[pl.ds(16, HOSTS), pl.ds(0, 128)]
    hit = (lane >> 2) == (cells & 31)
    covered = [
        jnp.max(jnp.where(hit & ((cells >> 5) == corner), 1, 0), axis=0, keepdims=True)
        for corner in range(4)
    ]

    def sheet(q, x):
        return half_ref[pl.ds((q * 16 + x % 16) * 16, 16)]

    for x in range(8):
        keep = jnp.where(top, covered[(x // 4) * 2], covered[(x // 4) * 2 + 1]) == 0
        number = now_ref[pl.ds((64 + x) * 16, 8), pl.ds(0, 128)]
        for q in range(4):
            center = sheet(q, x)
            laplace, advect = rate_parts(
                center,
                (sheet(q, x + 1), sheet(q, x - 1)),
                (sheet(q, x + 2), sheet(q, x - 2)),
                0,
                WIND_COARSE,
            )
            done = 0.5 * (
                now_ref[pl.ds((q * 16 + x) * 16, 8), pl.ds(0, 128)]
                + center[:8, :128]
                + number * laplace[:8, :128]
                - advect[:8, :128]
            )
            full_ref[q, x] = jnp.where(keep, done, 0.0)


def put_means(back, full_ref, cells_ref, table_ref, next_ref):
    even, odd = back[:, :128], back[:, 128:]
    values = jnp.concatenate(
        [even, pltpu.roll(even, 64, 1), odd, pltpu.roll(odd, 64, 1)], axis=0
    )
    high = values.astype(BF16)
    low, lowest = split(values - high.astype(F32))
    parts = jnp.concatenate([high, low, lowest, jnp.zeros_like(high)], axis=0)
    spread = dot_t(table_ref[COPY], parts)
    cells = cells_ref[pl.ds(8, 1)]
    row = lax.broadcasted_iota(jnp.int32, (256, 1), 0)
    corner = ((row >> 5) & 1) * 2 + ((row >> 2) & 1)
    spread = jnp.where((cells >> 5) == corner, spread, 0.0).astype(BF16)
    z = lax.broadcasted_iota(jnp.int32, (128, 256), 0)
    lane = lax.broadcasted_iota(jnp.int32, (128, 256), 1)
    here = ((z >> 2) == (cells & 31)) & ((z & 3) == ((lane >> 4) & 3)) & (cells >= 0)
    added = dot_t(spread, jnp.where(here, 1.0, 0.0).astype(BF16))
    for q in range(4):
        for x in range(8):
            at = (q * 8 + x) * 8
            next_ref[q, x] = full_ref[q, x] + added[at : at + 8]


def plane_parts(field, table_ref):
    both = dot(jnp.concatenate(split(field), axis=1), table_ref[PLANES])
    return both[:, :256], both[:, 256:]


def plus(left, right):
    if left is None or right is None:
        return right if left is None else left
    return left + right


def minus(left, right):
    if right is None:
        return left
    return -right if left is None else left - right


def x_parts(padded):
    laplace, advect = [], []
    for x in range(2, 18):
        near = minus(padded[x + 1], padded[x - 1])
        far = minus(padded[x + 2], padded[x - 2])
        laplace.append(plus(padded[x + 1], padded[x - 1]))
        near = None if near is None else (8.0 * WIND_PARTS[0]) * near
        far = None if far is None else WIND_PARTS[0] * far
        advect.append(minus(near, far))
    return laplace, advect


def plane(values, x):
    return values[x * HOSTS : (x + 1) * HOSTS]


def rate_of(numbers, padded, laplace, advect):
    x_laplace, x_advect = x_parts(padded)
    return [
        numbers[x] * plus(x_laplace[x], plane(laplace, x))
        - ADVECT_UNIT * plus(x_advect[x], plane(advect, x))
        for x in range(EDGE)
    ]


def means(planes, table_ref):
    sums = []
    for big_x in range(PB):
        group = planes[big_x * 4 : big_x * 4 + 4]
        sums.append((group[0] + group[1]) + (group[2] + group[3]))
    high, low = split(jnp.concatenate(sums, axis=0))
    every = dot(high, table_ref[MEAN]) + dot(low, table_ref[MEAN])
    lane_x = (lax.broadcasted_iota(jnp.int32, (HOSTS, 256), 1) >> 2) & 3
    total = plane(every, 0)
    for big_x in range(1, PB):
        total = jnp.where(lane_x == big_x, plane(every, big_x), total)
    return total


def lane_of_q():
    return (lax.broadcasted_iota(jnp.int32, (HOSTS, 256), 1) >> 4) & 3


def touch_kernel(fine_ref, number_ref, table_ref, after_hbm, out_ref):
    out_ref[...] = (
        fine_ref[pl.ds(0, 8)]
        + number_ref[pl.ds(0, 8), pl.ds(0, 128)]
        + table_ref[pl.ds(0, 16), pl.ds(0, 128)].astype(F32)[:8]
    )


def early_kernel(fields, fine_ref, number_ref, table_ref, after_hbm, step_ref, back_ref):
    numbers = [number_ref[:, pl.ds(x * 256, 256)] for x in range(EDGE)]
    nothing = [None, None]
    back = jnp.zeros((HOSTS, 256), F32)
    for q in fields:
        planes = []
        for x in range(EDGE):
            sides = [
                fine_ref[pl.ds((2 * x + side) * 4 + q, HOSTS, stride=128)] for side in range(2)
            ]
            planes.append(jnp.concatenate(sides, axis=1))
        parts = plane_parts(jnp.concatenate(planes, axis=0), table_ref)
        rate = rate_of(numbers, nothing + planes + nothing, *parts)
        half = [planes[x] + rate[x] for x in range(EDGE)]
        parts = plane_parts(jnp.concatenate(half, axis=0), table_ref)
        rate = rate_of(numbers, nothing + half + nothing, *parts)
        done = [0.5 * (planes[x] + half[x] + rate[x]) for x in range(EDGE)]
        for x in range(EDGE):
            step_ref[pl.ds(((q - fields[0]) * EDGE + x) * HOSTS, HOSTS)] = done[x]
        back = jnp.where(lane_of_q() == q, means(done, table_ref), back)
    back_ref[...] = back


def cells_kernel(route_ref, after_hbm, cells_ref):
    lane = lax.broadcasted_iota(jnp.int32, (8, 256), 1)
    row = lax.broadcasted_iota(jnp.int32, (HOSTS, 256), 0)
    by_eight = jnp.zeros((8, 256), jnp.int32)
    by_one = jnp.zeros((8, 256), jnp.int32)
    by_row = jnp.zeros((HOSTS, 256), jnp.int32)
    for slot in range(HOSTS):
        cell = route_ref[slot]
        by_eight = jnp.where(((lane >> 3) & 15) == slot, cell, by_eight)
        by_one = jnp.where((lane & 15) == slot, cell, by_one)
        by_row = jnp.where(row == slot, cell, by_row)
    cells_ref[pl.ds(0, 8)] = by_eight
    cells_ref[pl.ds(8, 8)] = by_one
    cells_ref[pl.ds(16, HOSTS)] = by_row


def ghosts(block_ref, q, t):
    interp = interp_table(PB, RATIO)
    first_half = lax.broadcasted_iota(jnp.int32, (HOSTS, 128), 1) < 64
    coarse = []
    for x in range(8):
        rows = block_ref[pl.ds(q * 8 + x, HOSTS, stride=SLOT_ROWS)]
        turned = pltpu.roll(rows, 64, 1)
        coarse.append(
            jnp.where(first_half, rows, turned) if t == 0 else jnp.where(first_half, turned, rows)
        )
    inner, outer = [], []
    for i in range(EDGE + 4):
        total = None
        for j in range(8):
            if interp[i, j] != 0.0:
                total = plus(total, float(interp[i, j]) * coarse[j])
        (inner if 2 <= i < EDGE + 2 else outer).append(total)
    inner = jnp.concatenate(split(jnp.concatenate(inner, axis=0)), axis=1)
    outer = jnp.concatenate(split(jnp.concatenate(outer, axis=0)), axis=1)
    return inner, outer


def ghost_part(block_ref, numbers, fields, table_ref):
    def planes_of(t):
        parts = [ghosts(block_ref, q, t) for q in fields]
        inner, outer = (jnp.concatenate(part, axis=0) for part in zip(*parts))
        return inner, dot(outer, table_ref[FACE])

    def rates(values, faces, both):
        result = []
        for i in range(len(fields)):
            low = [plane(faces, i * 4 + j) for j in range(2)]
            high = [plane(faces, i * 4 + j) for j in range(2, 4)]
            rows = both[i * 256 : (i + 1) * 256]
            result.append(
                rate_of(numbers, low + values[i] + high, rows[:, :256], rows[:, 256:])
            )
        return result

    inner, faces = planes_of(0)
    half = rates([[None] * EDGE for _ in fields], faces, dot(inner, table_ref[GHOST]))
    inner, faces = planes_of(1)
    stacked = jnp.concatenate([values for field in half for values in field], axis=0)
    operand = jnp.concatenate(split(stacked) + (inner,), axis=1)
    rate = rates(half, faces, dot(operand, table_ref[PLANES_AND_GHOST]))
    return [
        [0.5 * (half[i][x] + rate[i][x]) for x in range(EDGE)] for i in range(len(fields))
    ]


def last_kernel(
    got_ref,
    sent_hbm,
    step_hbm,
    old_hbm,
    number_hbm,
    full_ref,
    cells_ref,
    table_ref,
    fine_hbm,
    next_ref,
    sent_ref,
    step_ref,
    old_ref,
    number_ref,
    fine_ref,
    sems,
):
    copies = [
        pltpu.make_async_copy(src, dst, sems.at[i])
        for i, (src, dst) in enumerate(
            (
                (number_hbm, number_ref),
                (step_hbm, step_ref),
                (old_hbm, old_ref),
                (sent_hbm, sent_ref),
            )
        )
    ]
    for copy in copies:
        copy.start()

    def got(row):
        sides = [got_ref[pl.ds(row + side, HOSTS, stride=SLOT_ROWS)] for side in range(2)]
        return jnp.concatenate(sides, axis=1)

    placed = got_ref[pl.ds(FLAG_ROW, HOSTS, stride=SLOT_ROWS)] > 0.5
    copies[0].wait()
    numbers = [number_ref[:, pl.ds(x * 256, 256)] for x in range(EDGE)]
    added = []
    for q in range(4):
        if q % TOGETHER == 0:
            added += ghost_part(got_ref, numbers, range(q, q + TOGETHER), table_ref)
        if q == 0:
            for copy in copies[1:3]:
                copy.wait()
        for x in range(EDGE):
            done = step_ref[pl.ds((q * EDGE + x) * HOSTS, HOSTS)] + added[q][x]
            for side in range(2):
                at = pl.ds((2 * x + side) * 4 + q, HOSTS, stride=128)
                fine_ref[at] = jnp.where(
                    placed, done[:, side * 128 : side * 128 + 128], old_ref[at]
                )
    out = pltpu.make_async_copy(fine_ref, fine_hbm, sems.at[4])
    out.start()
    copies[3].wait()
    numbers = [got(NUMBER_ROW + 2 * x) for x in range(EDGE)]
    added = []
    back = jnp.zeros((HOSTS, 256), F32)
    for q in range(4):
        if q % TOGETHER == 0:
            added += ghost_part(sent_ref, numbers, range(q, q + TOGETHER), table_ref)
        back = jnp.where(lane_of_q() == q, means(added[q], table_ref), back)
    put_means(back + got(MEAN_ROW), full_ref, cells_ref, table_ref, next_ref)
    out.wait()


def call(kernel, operands, outs, smem=(), hbm=(), hbm_outs=(), scratch=(), flops=10**6, name=None):
    vmem = pl.BlockSpec(memory_space=pltpu.VMEM)
    scalar = pl.BlockSpec(memory_space=pltpu.SMEM)
    far = pl.BlockSpec(memory_space=pltpu.HBM)
    moved = sum(int(np.prod(o.shape)) * o.dtype.itemsize for o in operands)
    return pl.pallas_call(
        kernel,
        out_shape=tuple(jax.ShapeDtypeStruct(shape, dtype) for shape, dtype in outs),
        in_specs=[
            scalar if i in smem else far if i in hbm else vmem for i in range(len(operands))
        ],
        out_specs=tuple(far if i in hbm_outs else vmem for i in range(len(outs))),
        scratch_shapes=list(scratch),
        compiler_params=pltpu.CompilerParams(vmem_limit_bytes=LIMIT * 1024 * 1024),
        cost_estimate=pl.CostEstimate(flops=flops, bytes_accessed=moved, transcendentals=0),
        name=name,
    )(*operands)


def shards(coarse_state, diffusion_number, route_cell, fine_state, fine_diffusion):
    table = jnp.asarray(tables())
    fine_rows = fine_state.reshape(HOSTS, 4, 32, 128).transpose(0, 2, 1, 3).reshape(2048, 128)
    fine_numbers = fine_diffusion.reshape(HOSTS, EDGE**3)

    def swap(inner, outer, axis):
        count = lax.axis_size(axis)
        pairs = [[], []]
        for i in range(count - 1):
            pairs[i % 2] += [(i, i + 1), (i + 1, i)]
        return lax.ppermute(inner, axis, pairs[1]), lax.ppermute(outer, axis, pairs[0])

    fields = jnp.concatenate([coarse_state, diffusion_number[None]], axis=0)
    inner, outer = call(
        x_kernel,
        (fields[:, :4], fields[:, 4:]),
        [((5, 4, 8, 128), F32)] * 2,
        name="x_messages",
    )
    own = (inner, outer) + swap(inner, outer, "gx")

    def early(fields, after):
        return call(
            functools.partial(early_kernel, fields),
            (fine_rows, fine_numbers, table, after),
            [((len(fields) * 256, 256), F32), ((HOSTS, 256), F32)],
            hbm=(3,),
            flops=10**9,
            name="fine_early",
        )

    (touched,) = call(
        touch_kernel,
        (fine_rows, fine_numbers, table, own[2]),
        [((8, 128), F32)],
        hbm=(3,),
        name="touch",
    )
    low, high = call(
        y_kernel, own + (touched,), [((320, 128), F32)] * 2, hbm=(4,), name="y_messages"
    )
    everything, low, high = call(
        z_kernel,
        own + swap(low, high, "gy") + (touched,),
        [((1280, 128), F32), ((40, 128), F32), ((40, 128), F32)],
        hbm=(6,),
        name="z_messages",
    )
    step, back = early((0, 1, 2, 3), everything)
    far_low, far_high = swap(low, high, "gz")
    (cells,) = call(
        cells_kernel,
        (route_cell.reshape(HOSTS), everything),
        [((32, 256), jnp.int32)],
        smem=(0,),
        hbm=(1,),
        name="cells",
    )
    payload = (HOSTS * SLOT_ROWS, 128)
    sent, full = call(
        half_kernel,
        (everything, far_low, far_high, cells, fine_numbers, back),
        [(payload, F32), ((4, 8, 8, 128), F32)],
        hbm_outs=(0,),
        scratch=[
            pltpu.VMEM((1280, 256), F32),
            pltpu.VMEM((1024, 256), F32),
            pltpu.VMEM((512, 128), F32),
            pltpu.VMEM(payload, F32),
            pltpu.SemaphoreType.DMA,
        ],
        name="half_step",
    )
    got = lax.all_to_all(
        sent.reshape(HOSTS, SLOT_ROWS, 1, 128), "gz", split_axis=0, concat_axis=0, tiled=True
    ).reshape(payload)
    fine_done, coarse_next = call(
        last_kernel,
        (got, sent, step, fine_rows, fine_numbers, full, cells, table),
        [((2048, 128), F32), ((4, 8, 8, 128), F32)],
        hbm=(1, 2, 3, 4),
        hbm_outs=(0,),
        scratch=[
            pltpu.VMEM(payload, F32),
            pltpu.VMEM((1024, 256), F32),
            pltpu.VMEM((2048, 128), F32),
            pltpu.VMEM((HOSTS, 4096), F32),
            pltpu.VMEM((2048, 128), F32),
            pltpu.SemaphoreType.DMA((5,)),
        ],
        flops=10**9,
        name="last_step",
    )
    fine_next = (
        fine_done.reshape(HOSTS, 32, 4, 128).transpose(0, 2, 1, 3).reshape(fine_state.shape)
    )
    return coarse_next, fine_next


def solution(mesh):
    return jax.shard_map(
        shards,
        mesh=mesh,
        in_specs=(
            P(None, "gx", "gy", "gz"),
            P("gx", "gy", "gz"),
            P("gx", "gy", "gz", None),
            P("gx", "gy", "gz", None, None, None),
            P("gx", "gy", "gz", None, None),
        ),
        out_specs=(P(None, "gx", "gy", "gz"), P("gx", "gy", "gz", None, None, None)),
        check_vma=False,
    )
```
